256 devices in a mesh: row: 16 (over x, y_hi, core), col: 16 (over y_lo, z).
Axes of the slice: x: 4, y: 4 (y_hi: 2, y_lo: 2; y = y_hi * 2 + y_lo), z: 8, core: 2. Of those that a mesh axis runs over, the one named last changes fastest.
Arguments:
- x_matrix: float32 [16384, 16384], P('row', 'col'), as said below
- h_matrix: float32 [16384, 16384], P('row', 'col'), as said below
- x_mask: int32 [128, 128], P('row', 'col'), may hold values from 0 to 1, as said below
- h_mask: int32 [128, 128], P('row', 'col'), may hold values from 0 to 1, as said below
- panel: int32 [1], replicated, may hold values from 0 to 31
Outputs:
- congruence: float32 [512, 16384], P('row', 'col')
The draws below stay inside these ranges and needn't reach their ends.
Inputs may be any that keep to these rules, and one draw needn't show every extreme that they name: x_matrix is symmetric. h_matrix is symmetric. `x_mask`: symmetric 0/1 pattern with ones on the diagonal; most occupied blocks lie near the diagonal, with wrap around, or near the wrapped block distance 128 // 4, and a few other blocks are scattered. `h_mask`: symmetric 0/1 pattern with ones on the diagonal; most occupied blocks lie near the diagonal, with wrap around, or near the wrapped block distance 128 // 4, and a few other blocks are scattered.
All inputs are finite; a program needn't handle non-finite values.
Results may differ from the reference program's by a relative error of at most 0.000094.
Values sent between devices are 32-bit elements; how exact they have to be, the bound alone decides.
A program may use at most 64 MiB of HBM per device.

```python
import jax
import jax.numpy as jnp
from jax import lax

BLOCK_SIZE = 128
PANEL_BLOCKS = 4
BLOCKS = 128
ORDER = 16384
PANEL = 512


def symmetric_noise(key, scale):
    noise = jax.random.normal(key, (ORDER, ORDER), jnp.float32)
    return (noise + noise.T) * scale


def block_pattern(key):
    reach = jax.random.randint(key, (BLOCKS,), max(BLOCKS // 16, 1), max(BLOCKS // 8, 2) + 1)
    first = jnp.arange(BLOCKS)[:, None]
    second = jnp.arange(BLOCKS)[None, :]
    distance = jnp.abs(first - second)
    distance = jnp.minimum(distance, BLOCKS - distance)
    bound = jnp.minimum(reach[:, None], reach[None, :])
    nearby = distance <= bound
    planes = jnp.abs(distance - BLOCKS // 4) <= bound // 2
    scatter_draw = jax.random.randint(jax.random.fold_in(key, 11), (BLOCKS, BLOCKS), 0, 10)
    upper = (scatter_draw == 0) & (first < second)
    scattered = upper | upper.T
    return jnp.where(nearby | planes | scattered, 1, 0).astype(jnp.int32)


def draw_x_matrix(key, part):
    key = jax.random.fold_in(key, 1)
    return jnp.eye(ORDER, dtype=jnp.float32) + symmetric_noise(key, 0.35 / ORDER ** 0.5)


def draw_h_matrix(key, part):
    key = jax.random.fold_in(key, 2)
    diagonal = jax.random.uniform(jax.random.fold_in(key, 7), (ORDER,), jnp.float32, -2.0, 2.0)
    return jnp.eye(ORDER, dtype=jnp.float32) * diagonal[None, :] + symmetric_noise(key, 0.5 / ORDER ** 0.5)


def draw_x_mask(key, part):
    key = jax.random.fold_in(key, 3)
    return block_pattern(key)


def draw_h_mask(key, part):
    key = jax.random.fold_in(key, 4)
    return block_pattern(key)


def setup_inputs(seed: int = 0) -> dict:
    key_of = jax.random.split(jax.random.key(seed), 6)
    return {
        "x_matrix": draw_x_matrix(jax.random.fold_in(key_of[5], 71), 0),
        "h_matrix": draw_h_matrix(jax.random.fold_in(key_of[5], 71), 0),
        "x_mask": draw_x_mask(jax.random.fold_in(key_of[5], 71), 0),
        "h_mask": draw_h_mask(jax.random.fold_in(key_of[5], 71), 0),
        "panel": jax.random.randint(key_of[4], (1,), 0, BLOCKS // PANEL_BLOCKS).astype(jnp.int32),
    }


def expand(matrix, mask):
    grid = mask.astype(jnp.float32)[:, None, :, None]
    full = jnp.broadcast_to(grid, (BLOCKS, BLOCK_SIZE, BLOCKS, BLOCK_SIZE)).reshape(ORDER, ORDER)
    return matrix * full


def reference(x_matrix, h_matrix, x_mask, h_mask, panel):
    masked_x = expand(x_matrix, x_mask)
    masked_h = expand(h_matrix, h_mask)
    first = (panel[0] * PANEL).astype(jnp.int32)
    columns = lax.dynamic_slice_in_dim(masked_x, first, PANEL, 1)
    left = jnp.dot(columns.T, masked_h, precision=lax.Precision.HIGHEST, preferred_element_type=jnp.float32)
    return jnp.dot(left, masked_x, precision=lax.Precision.HIGHEST, preferred_element_type=jnp.float32)
```

```python
import functools

import jax
import jax.numpy as jnp
from jax import lax
from jax.experimental import pallas as pl
from jax.experimental.pallas import tpu as pltpu
from jax.sharding import PartitionSpec as P

MESH = pl.DeviceIdType.MESH
CHUNKS = 4
PANEL = 512
CHIPS = 8
RING = 8
EDGE = 128

DUE = {"A0": 0, "A1": 2, "A2": 6, "A3": 10, "A4": 12, "Z2": 15, "Z3": 18, "Z4": 21, "Z5": 24, "Z6": 27,
       "Z7": 30, "Z8": 33, "Z9": 36, "Z10": 38, "B1": 41, "B2": 45}
APART = 8
PREPARE = {"x_load": -1, "h_prep": 0.5, "x_prep": 11}

CORE_P, DIR_P, AG_P, CORE_R, CORE_O, DIR_O, YX = range(7)
RU, RD, GU, GD = 7, 11, 15, 19
N_SEMS = 23


def order():
    steps = [(t + APART * k, k, name) for k in range(CHUNKS) for name, t in DUE.items()]
    steps += [(t, -1, name) for name, t in PREPARE.items()]
    return [(name, k) for _, k, name in sorted(steps)]


def kernel(x_hbm, h_hbm, xm_ref, hm_ref, panel_ref, out_ref,
           xv, hv, xh, xl, hh, hl, wx, mx, mh, piece, pc, pr, rr, ab, tp, zu1, zd1, zu, zd, yr, tf,
           ob, oc, orv, load_sem, send, recv):
    row, col = lax.axis_index("row"), lax.axis_index("col")
    core, chip = lax.rem(row, 2), lax.div(row, 2)
    z, ylo = lax.rem(col, RING), lax.div(col, RING)
    sib = (row + 1 - 2 * core, col)
    ypart = (row, (1 - ylo) * RING + z)
    up = (row, ylo * RING + lax.rem(z + 1, RING))
    down = (row, ylo * RING + lax.rem(z + RING - 1, RING))

    def peer(d):
        return (lax.rem(chip + d, CHIPS) * 2 + core, col)

    def at_z(d):
        return lax.rem(z + (d + RING) % RING, RING)

    load_x = pltpu.make_async_copy(x_hbm, xv, load_sem.at[0])
    load_h = pltpu.make_async_copy(h_hbm, hv, load_sem.at[1])
    load_x.start()
    load_h.start()

    barrier = pltpu.get_barrier_semaphore()
    friends = [sib, ypart, up, down] + [peer(d) for d in range(1, CHIPS)]
    for friend in friends:
        pl.semaphore_signal(barrier, inc=1, device_id=friend, device_id_type=MESH)

    def remote(src, dst, k, sem, device):
        return pltpu.make_async_remote_copy(
            src_ref=src, dst_ref=dst, send_sem=send.at[k, sem], recv_sem=recv.at[k, sem],
            device_id=device, device_id_type=MESH)

    sent = []

    def push(src, dst, k, sem, device):
        copy = remote(src, dst, k, sem, device)
        copy.start()
        sent.append(copy)

    def spread(mask):
        m = mask.astype(jnp.float32)
        return jnp.concatenate(
            [jnp.broadcast_to(m[:, j:j + 1], (m.shape[0], EDGE)) for j in range(m.shape[1])], axis=1)

    def split(value):
        high = value.astype(jnp.bfloat16)
        return high, (value - high.astype(jnp.float32)).astype(jnp.bfloat16)

    def multiply(chunk, high, low, store, transposed):
        rows = chunk.shape[0]
        a, b = split(chunk)
        ab[0:rows, :] = a
        ab[rows:2 * rows, :] = b
        dims = (((1,), (1 if transposed else 0,)), ((), ()))

        def body(n, carry):
            cols = pl.ds(pl.multiple_of(n * 256, 256), 256)
            wh = high[cols, :] if transposed else high[:, cols]
            wl = low[cols, :] if transposed else low[:, cols]
            first = lax.dot_general(ab[...], wh, dims, preferred_element_type=jnp.float32)
            second = lax.dot_general(ab[0:rows, :], wl, dims, preferred_element_type=jnp.float32)
            store(cols, first[:rows] + (first[rows:] + second))
            return carry

        lax.fori_loop(0, high.shape[0] // 256, body, 0)

    def x_load():
        mx[...] = spread(xm_ref[...])
        s0 = jnp.where(panel_ref[0] == 2 * row, 1.0, 0.0)
        s1 = jnp.where(panel_ref[0] == 2 * row + 1, 1.0, 0.0)
        wx[0] = mx[0:4, :] * s0
        wx[1] = mx[4:8, :] * s1
        load_x.wait()

    def h_prep():
        mh[...] = spread(hm_ref[...])
        load_h.wait()

        def body(b, carry):
            rows = pl.ds(pl.multiple_of(b * EDGE, EDGE), EDGE)
            high, low = split(hv[rows, :] * mh[pl.ds(b, 1), :])
            hh[rows, :] = high
            hl[rows, :] = low
            return carry

        lax.fori_loop(0, 8, body, 0)

    def x_prep():
        def body(b, carry):
            rows = pl.ds(pl.multiple_of(b * EDGE, EDGE), EDGE)
            block = xv[lax.div(b, 4), pl.ds(lax.rem(b, 4) * 2, 2)].reshape(EDGE, 1024)
            high, low = split(block * mx[pl.ds(b, 1), :])
            xh[rows, :] = high
            xl[rows, :] = low
            return carry

        lax.fori_loop(0, 8, body, 0)

    def a0(k):
        for q in range(2):
            for g in range(CHIPS):
                w0, w1 = wx[0, g // 2:g // 2 + 1, :], wx[1, g // 2:g // 2 + 1, :]
                piece[k, q, g] = xv[0, g, q, k] * w0 + xv[1, g, q, k] * w1
        if k == 0:
            pl.semaphore_wait(barrier, len(friends))
        push(piece.at[k, 1 - core], pc.at[k], k, CORE_P, sib)

    def a1(k):
        remote(pc.at[k], pc.at[k], k, CORE_P, sib).wait_recv()
        piece[k, core] = piece[k, core] + pc[k]
        for d in range(1, CHIPS):
            remote(piece.at[k, core, lax.rem(chip + d, CHIPS)], pr.at[k, d - 1], k, DIR_P, peer(d)).start()
        sent.append(remote(pr.at[k], pr.at[k], k, DIR_P, sib))

    def a2(k):
        remote(pr.at[k], pr.at[k], k, DIR_P, sib).wait_recv()
        total = piece[k, core, chip]
        for d in range(CHIPS - 1):
            total = total + pr[k, d]
        rr[k, core, chip] = total
        for d in range(1, CHIPS):
            remote(rr.at[k, core, chip], rr.at[k, core, chip], k, AG_P, peer(d)).start()
        sent.append(remote(pr.at[k], pr.at[k], k, AG_P, sib))

    def a3(k):
        remote(pr.at[k], pr.at[k], k, AG_P, sib).wait_recv()
        push(rr.at[k, core], rr.at[k, core], k, CORE_R, sib)

    def a4(k):
        remote(rr.at[k, core], rr.at[k, 1 - core], k, CORE_R, sib).wait_recv()
        rows = PANEL // CHUNKS

        def store(cols, value):
            tp[k, :, :, cols] = value.reshape(RING, rows // RING, 256)

        multiply(rr[k].reshape(rows, 1024), hh, hl, store, True)
        push(tp.at[k, at_z(4), :, 0:512], zu1.at[k], k, RU, up)
        push(tp.at[k, at_z(4), :, 512:1024], zd1.at[k], k, RD, down)

    def z2(k):
        remote(zu1.at[k], zu1.at[k], k, RU, up).wait_recv()
        tp[k, at_z(3), :, 0:512] = tp[k, at_z(3), :, 0:512] + zu1[k]
        push(tp.at[k, at_z(3)], zu.at[k, 0], k, RU + 1, up)
        remote(zd1.at[k], zd1.at[k], k, RD, down).wait_recv()
        tp[k, at_z(-3), :, 512:1024] = tp[k, at_z(-3), :, 512:1024] + zd1[k]
        push(tp.at[k, at_z(-3)], zd.at[k, 0], k, RD + 1, down)

    def z_add(k, s):
        remote(zu.at[k, s], zu.at[k, s], k, RU + 1 + s, up).wait_recv()
        tp[k, at_z(2 - s)] = tp[k, at_z(2 - s)] + zu[k, s]
        push(tp.at[k, at_z(2 - s)], zu.at[k, s + 1], k, RU + 2 + s, up)
        remote(zd.at[k, s], zd.at[k, s], k, RD + 1 + s, down).wait_recv()
        tp[k, at_z(s - 2)] = tp[k, at_z(s - 2)] + zd[k, s]
        push(tp.at[k, at_z(s - 2)], zd.at[k, s + 1], k, RD + 2 + s, down)

    def z5(k):
        remote(zu.at[k, 2], zu.at[k, 2], k, RU + 3, up).wait_recv()
        remote(zd.at[k, 2], zd.at[k, 2], k, RD + 3, down).wait_recv()
        tp[k, z] = tp[k, z] + (zu[k, 2] + zd[k, 2])
        push(tp.at[k, z], yr.at[k], k, YX, ypart)

    def z6(k):
        remote(yr.at[k], yr.at[k], k, YX, ypart).wait_recv()
        tf[k, z] = tp[k, z] + yr[k]
        push(tf.at[k, z], tf.at[k, z], k, GU, up)
        push(tf.at[k, z], tf.at[k, z], k, GD, down)

    def z_pass(k, s):
        below, above = at_z(-s), at_z(s)
        remote(tf.at[k, below], tf.at[k, below], k, GU + s - 1, up).wait_recv()
        if s < 3:
            push(tf.at[k, below], tf.at[k, below], k, GU + s, up)
        else:
            push(tf.at[k, below, :, 0:512], tf.at[k, below, :, 0:512], k, GU + s, up)
        remote(tf.at[k, above], tf.at[k, above], k, GD + s - 1, down).wait_recv()
        if s < 3:
            push(tf.at[k, above], tf.at[k, above], k, GD + s, down)
        else:
            push(tf.at[k, above, :, 512:1024], tf.at[k, above, :, 512:1024], k, GD + s, down)

    def z10(k):
        far = at_z(4)
        remote(tf.at[k, far, :, 0:512], tf.at[k, far, :, 0:512], k, GU + 3, up).wait_recv()
        remote(tf.at[k, far, :, 512:1024], tf.at[k, far, :, 512:1024], k, GD + 3, down).wait_recv()
        rows = PANEL // CHUNKS

        def store(cols, value):
            ob[k, :, :, :, cols] = value.reshape(2, CHIPS, rows // 16, 256)

        multiply(tf[k].reshape(rows, 1024), xh, xl, store, False)
        push(ob.at[k, 1 - core], oc.at[k], k, CORE_O, sib)

    def b1(k):
        remote(oc.at[k], oc.at[k], k, CORE_O, sib).wait_recv()
        ob[k, core] = ob[k, core] + oc[k]
        for d in range(1, CHIPS):
            remote(ob.at[k, core, lax.rem(chip + d, CHIPS)], orv.at[k, d - 1], k, DIR_O, peer(d)).start()
        sent.append(remote(orv.at[k], orv.at[k], k, DIR_O, sib))

    def b2(k):
        remote(orv.at[k], orv.at[k], k, DIR_O, sib).wait_recv()
        total = ob[k, core, chip]
        for d in range(CHIPS - 1):
            total = total + orv[k, d]
        out_ref[k] = total

    stages = {
        "A0": a0, "A1": a1, "A2": a2, "A3": a3, "A4": a4, "Z2": z2,
        "Z3": lambda k: z_add(k, 0), "Z4": lambda k: z_add(k, 1), "Z5": z5, "Z6": z6,
        "Z7": lambda k: z_pass(k, 1), "Z8": lambda k: z_pass(k, 2), "Z9": lambda k: z_pass(k, 3),
        "Z10": z10, "B1": b1, "B2": b2,
        "x_load": lambda k: x_load(), "h_prep": lambda k: h_prep(), "x_prep": lambda k: x_prep(),
    }
    for name, k in order():
        stages[name](k)
    for copy in sent:
        copy.wait_send()


def on_device(x_matrix, h_matrix, x_mask, h_mask, panel):
    n, slab = x_matrix.shape[0], 32 // CHUNKS
    group = PANEL // CHUNKS // RING
    f32, bf16 = jnp.float32, jnp.bfloat16
    vmem, hbm = pl.BlockSpec(memory_space=pltpu.VMEM), pl.BlockSpec(memory_space=pl.ANY)
    out = pl.pallas_call(
        kernel,
        out_shape=jax.ShapeDtypeStruct((CHUNKS, slab, n), f32),
        in_specs=[hbm, hbm, vmem, vmem, pl.BlockSpec(memory_space=pltpu.SMEM)],
        out_specs=vmem,
        scratch_shapes=[
            pltpu.VMEM((2, CHIPS, 2, CHUNKS, slab, n), f32),
            pltpu.VMEM((n, n), f32),
            pltpu.VMEM((n, n), bf16), pltpu.VMEM((n, n), bf16),
            pltpu.VMEM((n, n), bf16), pltpu.VMEM((n, n), bf16),
            pltpu.VMEM((2, 4, n), f32), pltpu.VMEM((8, n), f32), pltpu.VMEM((8, n), f32),
            pltpu.VMEM((CHUNKS, 2, CHIPS, slab, n), f32),
            pltpu.VMEM((CHUNKS, CHIPS, slab, n), f32),
            pltpu.VMEM((CHUNKS, CHIPS - 1, slab, n), f32),
            pltpu.VMEM((CHUNKS, 2, CHIPS, slab, n), f32),
            pltpu.VMEM((2 * PANEL // CHUNKS, n), bf16),
            pltpu.VMEM((CHUNKS, RING, group, n), f32),
            pltpu.VMEM((CHUNKS, group, n // 2), f32), pltpu.VMEM((CHUNKS, group, n // 2), f32),
            pltpu.VMEM((CHUNKS, 3, group, n), f32), pltpu.VMEM((CHUNKS, 3, group, n), f32),
            pltpu.VMEM((CHUNKS, group, n), f32),
            pltpu.VMEM((CHUNKS, RING, group, n), f32),
            pltpu.VMEM((CHUNKS, 2, CHIPS, slab, n), f32),
            pltpu.VMEM((CHUNKS, CHIPS, slab, n), f32),
            pltpu.VMEM((CHUNKS, CHIPS - 1, slab, n), f32),
            pltpu.SemaphoreType.DMA((2,)),
            pltpu.SemaphoreType.DMA((CHUNKS, N_SEMS)),
            pltpu.SemaphoreType.DMA((CHUNKS, N_SEMS)),
        ],
        compiler_params=pltpu.CompilerParams(
            collective_id=0, has_side_effects=True, vmem_limit_bytes=56 * 1024 * 1024),
    )(x_matrix.reshape(2, CHIPS, 2, CHUNKS, slab, n), h_matrix, x_mask, h_mask, panel)
    return out.reshape(32, n)


def solution(mesh):
    return jax.shard_map(
        on_device,
        mesh=mesh,
        in_specs=(P("row", "col"), P("row", "col"), P("row", "col"), P("row", "col"), P()),
        out_specs=P("row", "col"),
        check_vma=False,
    )
```

```python
import functools

import jax
import jax.numpy as jnp
from jax import lax
from jax.experimental import pallas as pl
from jax.experimental.pallas import tpu as pltpu
from jax.sharding import PartitionSpec as P

MESH = pl.DeviceIdType.MESH
CHUNKS = 4
PANEL = 512
ROWS = PANEL // CHUNKS
CHIPS = 8
RING = 8
EDGE = 128

ORDER = (
    ("x_load", 0), ("A0", 0), ("A0", 1), ("A1", 0), ("A0", 2), ("A1", 1), ("A1", 2), ("A0", 3), ("h_prep", 0),
    ("A2", 0), ("A1", 3), ("x_prep", 0), ("A2", 2), ("A2", 1), ("A3", 0), ("A4", 0), ("A4b", 0), ("A2", 3),
    ("Z2", 0), ("A3", 2), ("A4", 2), ("A3", 1), ("A4b", 2), ("Z3", 0), ("A4", 1), ("A4b", 1), ("Z2", 2),
    ("A3", 3), ("A4", 3), ("Z2", 1), ("A4b", 3), ("Z3", 2), ("Z4", 0), ("Z2", 3), ("Z3", 1), ("Z4", 2), ("Z6", 0),
    ("Z3", 3), ("Z4", 1), ("Z6", 2), ("Z7", 0), ("P1", 0), ("Z4", 3), ("Z6", 1), ("Z7", 2), ("P1", 2), ("Z8", 0),
    ("P2", 0), ("Z6", 3), ("Z7", 1), ("P1", 1), ("Z8", 2), ("P2", 2), ("Z9", 0), ("P3", 0), ("Z7", 3), ("P1", 3),
    ("Z8", 1), ("P2", 1), ("Z9", 2), ("P3", 2), ("Z11", 0), ("Z8", 3), ("P2", 3), ("B1", 0), ("Z9", 1), ("P3", 1),
    ("Z11", 2), ("B1", 2), ("Z9", 3), ("P3", 3), ("Z11", 1), ("B1", 1), ("Z11", 3), ("B1", 3), ("B2", 1),
    ("B2", 2), ("B2", 0), ("B2", 3),
)

CORE_P, DIR_P, AG_P, CORE_R, CORE_O, DIR_O, LAST, FIRST = range(8)
RU, RD, GU, GD = 8, 11, 14, 17
N_SEMS = 20


def kernel(x_hbm, h_hbm, xm_ref, hm_ref, panel_ref, out_ref,
           xv, hv, xh, xl, hh, hl, wx, mx, mh, piece, pc, pr, rr, ab, tb, tp, zu1, zd1, zu, zd, zl, tf,
           ob, oc, orv, load_sem, send, recv):
    row, col = lax.axis_index("row"), lax.axis_index("col")
    core, chip = lax.rem(row, 2), lax.div(row, 2)
    z, ylo = lax.rem(col, RING), lax.div(col, RING)
    sib = (row + 1 - 2 * core, col)
    other = 1 - ylo
    ypart = (row, other * RING + z)
    z_up, z_down = lax.rem(z + 1, RING), lax.rem(z + RING - 1, RING)
    up, up_other = (row, ylo * RING + z_up), (row, other * RING + z_up)
    down, down_other = (row, ylo * RING + z_down), (row, other * RING + z_down)
    around = [up, down, up_other, down_other, ypart]

    def peer(d):
        return (lax.rem(chip + d, CHIPS) * 2 + core, col)

    def at_z(d):
        return lax.rem(z + (d + RING) % RING, RING)

    load_x = pltpu.make_async_copy(x_hbm, xv, load_sem.at[0])
    load_h = pltpu.make_async_copy(h_hbm, hv, load_sem.at[1])
    load_x.start()

    barrier = pltpu.get_barrier_semaphore()
    friends = [sib] + around + [peer(d) for d in range(1, CHIPS)]
    for friend in friends:
        pl.semaphore_signal(barrier, inc=1, device_id=friend, device_id_type=MESH)

    def remote(src, dst, k, sem, device):
        return pltpu.make_async_remote_copy(
            src_ref=src, dst_ref=dst, send_sem=send.at[k, sem], recv_sem=recv.at[k, sem],
            device_id=device, device_id_type=MESH)

    sent = []

    def push(src, dst, k, sem, device):
        copy = remote(src, dst, k, sem, device)
        copy.start()
        sent.append(copy)

    def spread(mask):
        m = mask.astype(jnp.float32)
        return jnp.concatenate(
            [jnp.broadcast_to(m[:, j:j + 1], (m.shape[0], EDGE)) for j in range(m.shape[1])], axis=1)

    def split(value):
        high = value.astype(jnp.bfloat16)
        return high, (value - high.astype(jnp.float32)).astype(jnp.bfloat16)

    def product_one(k, step):
        far = lax.div(at_z(4), 2)
        turn = 1 - 2 * lax.rem(z + 1, 2)
        pair = lax.rem(far + (0, 4 + turn, 4 - turn, 2)[step], 4)
        rows = pl.ds(pl.multiple_of(pair * 256, 256), 256)
        dims = (((1,), (1,)), ((), ()))
        first = lax.dot_general(ab[k], hh[rows, :], dims, preferred_element_type=jnp.float32)
        second = lax.dot_general(ab[k, 0:ROWS, :], hl[rows, :], dims, preferred_element_type=jnp.float32)
        value = first[:ROWS] + (first[ROWS:] + second)
        tp[k, 2 * pair] = value[:, :EDGE].reshape(2, ROWS // 2, EDGE)
        tp[k, 2 * pair + 1] = value[:, EDGE:].reshape(2, ROWS // 2, EDGE)

    def product_two(k, step):
        turn = 1 - 2 * lax.rem(z + 1, 2)
        pair = lax.rem(lax.div(z, 2) + (0, 4 + turn, 4 - turn, 2)[step], 4)
        for half in range(2):
            a, b = split(tf[k, 2 * pair + half].reshape(ROWS, EDGE))
            tb[0:ROWS, half * EDGE:(half + 1) * EDGE] = a
            tb[ROWS:, half * EDGE:(half + 1) * EDGE] = b
        rows = pl.ds(pl.multiple_of(pair * 256, 256), 256)
        for n in range(0, 1024, 256):
            first = jnp.dot(tb[...], xh[rows, n:n + 256], preferred_element_type=jnp.float32)
            second = jnp.dot(tb[0:ROWS, :], xl[rows, n:n + 256], preferred_element_type=jnp.float32)
            value = (first[:ROWS] + (first[ROWS:] + second)).reshape(2, CHIPS, ROWS // 16, 256)
            ob[k, :, :, :, n:n + 256] = value if step == 0 else ob[k, :, :, :, n:n + 256] + value

    def x_load():
        mx[...] = spread(xm_ref[...])
        s0 = jnp.where(panel_ref[0] == 2 * row, 1.0, 0.0)
        s1 = jnp.where(panel_ref[0] == 2 * row + 1, 1.0, 0.0)
        wx[0] = mx[0:4, :] * s0
        wx[1] = mx[4:8, :] * s1
        load_x.wait()
        load_h.start()

    def h_prep():
        mh[...] = spread(hm_ref[...])
        load_h.wait()

        def body(b, carry):
            rows = pl.ds(pl.multiple_of(b * EDGE, EDGE), EDGE)
            high, low = split(hv[rows, :] * mh[pl.ds(b, 1), :])
            hh[rows, :] = high
            hl[rows, :] = low
            return carry

        lax.fori_loop(0, 8, body, 0)

    def x_prep():
        def body(b, carry):
            rows = pl.ds(pl.multiple_of(b * EDGE, EDGE), EDGE)
            block = xv[lax.div(b, 4), pl.ds(lax.rem(b, 4) * 2, 2)].reshape(EDGE, 1024)
            high, low = split(block * mx[pl.ds(b, 1), :])
            xh[rows, :] = high
            xl[rows, :] = low
            return carry

        lax.fori_loop(0, 8, body, 0)

    def a0(k):
        for q in range(2):
            for g in range(CHIPS):
                w0, w1 = wx[0, g // 2:g // 2 + 1, :], wx[1, g // 2:g // 2 + 1, :]
                piece[k, q, g] = xv[0, g, q, k] * w0 + xv[1, g, q, k] * w1
        if not sent:
            pl.semaphore_wait(barrier, len(friends))
        push(piece.at[k, 1 - core], pc.at[k], k, CORE_P, sib)

    def a1(k):
        remote(pc.at[k], pc.at[k], k, CORE_P, sib).wait_recv()
        piece[k, core] = piece[k, core] + pc[k]
        for d in range(1, CHIPS):
            remote(piece.at[k, core, lax.rem(chip + d, CHIPS)], pr.at[k, d - 1], k, DIR_P, peer(d)).start()
        sent.append(remote(pr.at[k], pr.at[k], k, DIR_P, sib))

    def a2(k):
        remote(pr.at[k], pr.at[k], k, DIR_P, sib).wait_recv()
        total = piece[k, core, chip]
        for d in range(CHIPS - 1):
            total = total + pr[k, d]
        rr[k, core, chip] = total
        for d in range(1, CHIPS):
            remote(rr.at[k, core, chip], rr.at[k, core, chip], k, AG_P, peer(d)).start()
        sent.append(remote(pr.at[k], pr.at[k], k, AG_P, sib))

    def a3(k):
        remote(pr.at[k], pr.at[k], k, AG_P, sib).wait_recv()
        push(rr.at[k, core], rr.at[k, core], k, CORE_R, sib)

    def a4(k):
        remote(rr.at[k, core], rr.at[k, 1 - core], k, CORE_R, sib).wait_recv()
        high, low = split(rr[k].reshape(ROWS, 1024))
        ab[k, 0:ROWS, :] = high
        ab[k, ROWS:, :] = low
        product_one(k, 0)
        push(tp.at[k, at_z(4), 0], zu1.at[k], k, RU, up)
        push(tp.at[k, at_z(4), 1], zd1.at[k], k, RD, down)

    def a4b(k):
        for step in (1, 2, 3):
            product_one(k, step)
        remote(tp.at[k, z, other], zl.at[k, 4], k, LAST, ypart).start()

    def z2(k):
        remote(zu1.at[k], zu1.at[k], k, RU, up).wait_recv()
        tp[k, at_z(3), 0] = tp[k, at_z(3), 0] + zu1[k]
        push(tp.at[k, at_z(3)], zu.at[k, 0], k, RU + 1, up)
        remote(zd1.at[k], zd1.at[k], k, RD, down).wait_recv()
        tp[k, at_z(-3), 1] = tp[k, at_z(-3), 1] + zd1[k]
        push(tp.at[k, at_z(-3)], zd.at[k, 0], k, RD + 1, down)

    def z3(k):
        remote(zu.at[k, 0], zu.at[k, 0], k, RU + 1, up).wait_recv()
        tp[k, at_z(2)] = tp[k, at_z(2)] + zu[k, 0]
        push(tp.at[k, at_z(2)], zu.at[k, 1], k, RU + 2, up)
        remote(zd.at[k, 0], zd.at[k, 0], k, RD + 1, down).wait_recv()
        tp[k, at_z(-2)] = tp[k, at_z(-2)] + zd[k, 0]
        push(tp.at[k, at_z(-2)], zd.at[k, 1], k, RD + 2, down)

    def z4(k):
        remote(zu.at[k, 1], zu.at[k, 1], k, RU + 2, up).wait_recv()
        tp[k, z_up] = tp[k, z_up] + zu[k, 1]
        remote(tp.at[k, z_up, other], zl.at[k, 2], k, LAST, up_other).start()
        remote(tp.at[k, z_up, ylo], zl.at[k, 0], k, LAST, up).start()
        remote(zd.at[k, 1], zd.at[k, 1], k, RD + 2, down).wait_recv()
        tp[k, z_down] = tp[k, z_down] + zd[k, 1]
        remote(tp.at[k, z_down, other], zl.at[k, 3], k, LAST, down_other).start()
        remote(tp.at[k, z_down, ylo], zl.at[k, 1], k, LAST, down).start()
        sent.append(remote(zl.at[k], zl.at[k], k, LAST, up))

    def z6(k):
        remote(zl.at[k], zl.at[k], k, LAST, up).wait_recv()
        total = tp[k, z, ylo]
        for d in range(5):
            total = total + zl[k, d]
        tf[k, z, ylo] = total
        for device in (up_other, down_other, up, down, ypart):
            remote(tf.at[k, z, ylo], tf.at[k, z, ylo], k, FIRST, device).start()
        sent.append(remote(zl.at[k], zl.at[k], k, FIRST, up))

    def z7(k):
        remote(zl.at[k], zl.at[k], k, FIRST, up).wait_recv()
        push(tf.at[k, z_down], tf.at[k, z_down], k, GU, up)
        push(tf.at[k, z_up], tf.at[k, z_up], k, GD, down)

    def z8(k):
        below, above = at_z(-2), at_z(2)
        remote(tf.at[k, below], tf.at[k, below], k, GU, up).wait_recv()
        push(tf.at[k, below], tf.at[k, below], k, GU + 1, up)
        remote(tf.at[k, above], tf.at[k, above], k, GD, down).wait_recv()
        push(tf.at[k, above], tf.at[k, above], k, GD + 1, down)

    def z9(k):
        below, above = at_z(-3), at_z(3)
        remote(tf.at[k, below], tf.at[k, below], k, GU + 1, up).wait_recv()
        push(tf.at[k, below, 0], tf.at[k, below, 0], k, GU + 2, up)
        remote(tf.at[k, above], tf.at[k, above], k, GD + 1, down).wait_recv()
        push(tf.at[k, above, 1], tf.at[k, above, 1], k, GD + 2, down)

    def z11(k):
        far = at_z(4)
        remote(tf.at[k, far, 0], tf.at[k, far, 0], k, GU + 2, up).wait_recv()
        remote(tf.at[k, far, 1], tf.at[k, far, 1], k, GD + 2, down).wait_recv()
        product_two(k, 3)
        push(ob.at[k, 1 - core], oc.at[k], k, CORE_O, sib)

    def b1(k):
        remote(oc.at[k], oc.at[k], k, CORE_O, sib).wait_recv()
        ob[k, core] = ob[k, core] + oc[k]
        for d in range(1, CHIPS):
            remote(ob.at[k, core, lax.rem(chip + d, CHIPS)], orv.at[k, d - 1], k, DIR_O, peer(d)).start()
        sent.append(remote(orv.at[k], orv.at[k], k, DIR_O, sib))

    def b2(k):
        remote(orv.at[k], orv.at[k], k, DIR_O, sib).wait_recv()
        total = ob[k, core, chip]
        for d in range(CHIPS - 1):
            total = total + orv[k, d]
        out_ref[k] = total

    stages = {
        "A0": a0, "A1": a1, "A2": a2, "A3": a3, "A4": a4, "A4b": a4b, "Z2": z2, "Z3": z3, "Z4": z4, "Z6": z6,
        "Z7": z7, "P1": lambda k: product_two(k, 0), "Z8": z8, "P2": lambda k: product_two(k, 1),
        "Z9": z9, "P3": lambda k: product_two(k, 2), "Z11": z11, "B1": b1, "B2": b2,
        "x_load": lambda k: x_load(), "h_prep": lambda k: h_prep(), "x_prep": lambda k: x_prep(),
    }
    for name, k in ORDER:
        stages[name](k)
    for copy in sent:
        copy.wait_send()


def on_device(x_matrix, h_matrix, x_mask, h_mask, panel):
    n, slab = x_matrix.shape[0], 32 // CHUNKS
    part = (ROWS // 2, EDGE)
    f32, bf16 = jnp.float32, jnp.bfloat16
    vmem, hbm = pl.BlockSpec(memory_space=pltpu.VMEM), pl.BlockSpec(memory_space=pl.ANY)
    out = pl.pallas_call(
        kernel,
        out_shape=jax.ShapeDtypeStruct((CHUNKS, slab, n), f32),
        in_specs=[hbm, hbm, vmem, vmem, pl.BlockSpec(memory_space=pltpu.SMEM)],
        out_specs=vmem,
        scratch_shapes=[
            pltpu.VMEM((2, CHIPS, 2, CHUNKS, slab, n), f32),
            pltpu.VMEM((n, n), f32),
            pltpu.VMEM((n, n), bf16), pltpu.VMEM((n, n), bf16),
            pltpu.VMEM((n, n), bf16), pltpu.VMEM((n, n), bf16),
            pltpu.VMEM((2, 4, n), f32), pltpu.VMEM((8, n), f32), pltpu.VMEM((8, n), f32),
            pltpu.VMEM((CHUNKS, 2, CHIPS, slab, n), f32),
            pltpu.VMEM((CHUNKS, CHIPS, slab, n), f32),
            pltpu.VMEM((CHUNKS, CHIPS - 1, slab, n), f32),
            pltpu.VMEM((CHUNKS, 2, CHIPS, slab, n), f32),
            pltpu.VMEM((CHUNKS, 2 * ROWS, n), bf16), pltpu.VMEM((2 * ROWS, 2 * EDGE), bf16),
            pltpu.VMEM((CHUNKS, RING, 2, *part), f32),
            pltpu.VMEM((CHUNKS, *part), f32), pltpu.VMEM((CHUNKS, *part), f32),
            pltpu.VMEM((CHUNKS, 2, 2, *part), f32), pltpu.VMEM((CHUNKS, 2, 2, *part), f32),
            pltpu.VMEM((CHUNKS, 5, *part), f32),
            pltpu.VMEM((CHUNKS, RING, 2, *part), f32),
            pltpu.VMEM((CHUNKS, 2, CHIPS, slab, n), f32),
            pltpu.VMEM((CHUNKS, CHIPS, slab, n), f32),
            pltpu.VMEM((CHUNKS, CHIPS - 1, slab, n), f32),
            pltpu.SemaphoreType.DMA((2,)),
            pltpu.SemaphoreType.DMA((CHUNKS, N_SEMS)),
            pltpu.SemaphoreType.DMA((CHUNKS, N_SEMS)),
        ],
        compiler_params=pltpu.CompilerParams(
            collective_id=0, has_side_effects=True, vmem_limit_bytes=56 * 1024 * 1024),
    )(x_matrix.reshape(2, CHIPS, 2, CHUNKS, slab, n), h_matrix, x_mask, h_mask, panel)
    return out.reshape(32, n)


def solution(mesh):
    return jax.shard_map(
        on_device,
        mesh=mesh,
        in_specs=(P("row", "col"), P("row", "col"), P("row", "col"), P("row", "col"), P()),
        out_specs=P("row", "col"),
        check_vma=False,
    )
```

```python
import functools

import jax
import jax.numpy as jnp
from jax import lax
from jax.experimental import pallas as pl
from jax.experimental.pallas import tpu as pltpu
from jax.sharding import PartitionSpec as P

MESH = pl.DeviceIdType.MESH
CHUNKS = 4
PANEL = 512
ROWS = PANEL // CHUNKS
CHIPS = 8
RING = 8
EDGE = 128

ORDER = (
    ("x_load", 0), ("A0", 2), ("A0", 3), ("A0", 1), ("A1", 2), ("A1", 3), ("A1", 1), ("A0", 0), ("A1", 0),
    ("A2", 2), ("A2", 3), ("A2", 1), ("h_prep", 0), ("A2", 0), ("x_prep", 0), ("A3", 2), ("A4", 2), ("A4b", 2),
    ("A3", 3), ("A4", 3), ("Z2", 2), ("A3", 1), ("A4b", 3), ("A4", 1), ("A4b", 1), ("A3", 0), ("Z2", 3),
    ("Z3", 2), ("A4", 0), ("Z2", 1), ("A4b", 0), ("Z3", 3), ("Z4", 2), ("Z2", 0), ("Z3", 1), ("Z4", 3), ("Z6", 2),
    ("Z3", 0), ("Z4", 1), ("Z6", 3), ("Z7", 2), ("Z4", 0), ("Z6", 1), ("Z7", 3), ("Z8", 2), ("P1", 2), ("Z6", 0),
    ("Z7", 1), ("Z8", 3), ("P1", 3), ("Z9", 2), ("P2", 2), ("Z7", 0), ("P3", 2), ("Z8", 1), ("P1", 1), ("Z11", 2),
    ("Z9", 3), ("P2", 3), ("P3", 3), ("B1", 2), ("Z8", 0), ("P1", 0), ("Z9", 1), ("P2", 1), ("P3", 1), ("Z11", 3),
    ("B1", 3), ("Z9", 0), ("P2", 0), ("Z11", 1), ("B2", 2), ("B1", 1), ("P3", 0), ("Z11", 0), ("B1", 0),
    ("B2", 3), ("B2", 0), ("B2", 1),
)

CORE_P, DIR_P, AG_P, CORE_R, CORE_O, DIR_O, OWN, HALF_U, HALF_D, LAST, FIRST, NEAR, PASS_U, PASS_D = range(14)
RU, RD, GU, GD = 14, 16, 18, 20
N_SEMS = 22


def kernel(x_hbm, h_hbm, xm_ref, hm_ref, panel_ref, out_ref,
           xv, hv, xh, xl, hh, hl, wx, mx, mh, piece, pc, pr, rr, ab, tb, tp, zu1, zd1, zu, zd, zhu, zhd, zl, yo, tf,
           ob, oc, orv, load_sem, send, recv):
    row, col = lax.axis_index("row"), lax.axis_index("col")
    core, chip = lax.rem(row, 2), lax.div(row, 2)
    z, ylo = lax.rem(col, RING), lax.div(col, RING)
    sib = (row + 1 - 2 * core, col)
    other = 1 - ylo
    ypart = (row, other * RING + z)
    z_up, z_down = lax.rem(z + 1, RING), lax.rem(z + RING - 1, RING)
    up, up_other = (row, ylo * RING + z_up), (row, other * RING + z_up)
    down, down_other = (row, ylo * RING + z_down), (row, other * RING + z_down)
    around = [up, down, up_other, down_other, ypart]

    def peer(d):
        return (lax.rem(chip + d, CHIPS) * 2 + core, col)

    def at_z(d):
        return lax.rem(z + (d + RING) % RING, RING)

    load_x = pltpu.make_async_copy(x_hbm, xv, load_sem.at[0])
    load_h = pltpu.make_async_copy(h_hbm, hv, load_sem.at[1])
    load_x.start()

    barrier = pltpu.get_barrier_semaphore()
    friends = [sib] + around + [peer(d) for d in range(1, CHIPS)]
    for friend in friends:
        pl.semaphore_signal(barrier, inc=1, device_id=friend, device_id_type=MESH)

    def remote(src, dst, k, sem, device):
        return pltpu.make_async_remote_copy(
            src_ref=src, dst_ref=dst, send_sem=send.at[k, sem], recv_sem=recv.at[k, sem],
            device_id=device, device_id_type=MESH)

    sent = []

    def push(src, dst, k, sem, device):
        copy = remote(src, dst, k, sem, device)
        copy.start()
        sent.append(copy)

    def spread(mask):
        m = mask.astype(jnp.float32)
        return jnp.concatenate(
            [jnp.broadcast_to(m[:, j:j + 1], (m.shape[0], EDGE)) for j in range(m.shape[1])], axis=1)

    def split(value):
        high = value.astype(jnp.bfloat16)
        return high, (value - high.astype(jnp.float32)).astype(jnp.bfloat16)

    def product_one(k, step):
        far = lax.div(at_z(4), 2)
        turn = 1 - 2 * lax.rem(z + 1, 2)
        pair = lax.rem(far + (0, 4 + turn, 4 - turn, 2)[step], 4)
        rows = pl.ds(pl.multiple_of(pair * 256, 256), 256)
        dims = (((1,), (1,)), ((), ()))
        first = lax.dot_general(ab[k], hh[rows, :], dims, preferred_element_type=jnp.float32)
        second = lax.dot_general(ab[k, 0:ROWS, :], hl[rows, :], dims, preferred_element_type=jnp.float32)
        value = first[:ROWS] + (first[ROWS:] + second)
        tp[k, 2 * pair] = value[:, :EDGE].reshape(2, ROWS // 2, EDGE)
        tp[k, 2 * pair + 1] = value[:, EDGE:].reshape(2, ROWS // 2, EDGE)

    def product_two(k, step):
        turn = 1 - 2 * lax.rem(z + 1, 2)
        pair = lax.rem(lax.div(z, 2) + (0, 4 + turn, 4 - turn, 2)[step], 4)
        for half in range(2):
            a, b = split(tf[k, 2 * pair + half].reshape(ROWS, EDGE))
            tb[0:ROWS, half * EDGE:(half + 1) * EDGE] = a
            tb[ROWS:, half * EDGE:(half + 1) * EDGE] = b
        rows = pl.ds(pl.multiple_of(pair * 256, 256), 256)
        for n in range(0, 1024, 256):
            first = jnp.dot(tb[...], xh[rows, n:n + 256], preferred_element_type=jnp.float32)
            second = jnp.dot(tb[0:ROWS, :], xl[rows, n:n + 256], preferred_element_type=jnp.float32)
            value = (first[:ROWS] + (first[ROWS:] + second)).reshape(2, CHIPS, ROWS // 16, 256)
            ob[k, :, :, :, n:n + 256] = value if step == 0 else ob[k, :, :, :, n:n + 256] + value

    def x_load():
        mx[...] = spread(xm_ref[...])
        s0 = jnp.where(panel_ref[0] == 2 * row, 1.0, 0.0)
        s1 = jnp.where(panel_ref[0] == 2 * row + 1, 1.0, 0.0)
        wx[0] = mx[0:4, :] * s0
        wx[1] = mx[4:8, :] * s1
        load_x.wait()
        load_h.start()

    def h_prep():
        mh[...] = spread(hm_ref[...])
        load_h.wait()

        def body(b, carry):
            rows = pl.ds(pl.multiple_of(b * EDGE, EDGE), EDGE)
            high, low = split(hv[rows, :] * mh[pl.ds(b, 1), :])
            hh[rows, :] = high
            hl[rows, :] = low
            return carry

        lax.fori_loop(0, 8, body, 0)

    def x_prep():
        def body(b, carry):
            rows = pl.ds(pl.multiple_of(b * EDGE, EDGE), EDGE)
            block = xv[lax.div(b, 4), pl.ds(lax.rem(b, 4) * 2, 2)].reshape(EDGE, 1024)
            high, low = split(block * mx[pl.ds(b, 1), :])
            xh[rows, :] = high
            xl[rows, :] = low
            return carry

        lax.fori_loop(0, 8, body, 0)

    def a0(k):
        for q in range(2):
            for g in range(CHIPS):
                w0, w1 = wx[0, g // 2:g // 2 + 1, :], wx[1, g // 2:g // 2 + 1, :]
                piece[k, q, g] = xv[0, g, q, k] * w0 + xv[1, g, q, k] * w1
        if not sent:
            pl.semaphore_wait(barrier, len(friends))
        push(piece.at[k, 1 - core], pc.at[k], k, CORE_P, sib)

    def a1(k):
        remote(pc.at[k], pc.at[k], k, CORE_P, sib).wait_recv()
        piece[k, core] = piece[k, core] + pc[k]
        for d in range(1, CHIPS):
            remote(piece.at[k, core, lax.rem(chip + d, CHIPS)], pr.at[k, d - 1], k, DIR_P, peer(d)).start()
        sent.append(remote(pr.at[k], pr.at[k], k, DIR_P, sib))

    def a2(k):
        remote(pr.at[k], pr.at[k], k, DIR_P, sib).wait_recv()
        total = piece[k, core, chip]
        for d in range(CHIPS - 1):
            total = total + pr[k, d]
        rr[k, core, chip] = total
        for d in range(1, CHIPS):
            remote(rr.at[k, core, chip], rr.at[k, core, chip], k, AG_P, peer(d)).start()
        sent.append(remote(pr.at[k], pr.at[k], k, AG_P, sib))

    def a3(k):
        remote(pr.at[k], pr.at[k], k, AG_P, sib).wait_recv()
        push(rr.at[k, core], rr.at[k, core], k, CORE_R, sib)

    def a4(k):
        remote(rr.at[k, core], rr.at[k, 1 - core], k, CORE_R, sib).wait_recv()
        high, low = split(rr[k].reshape(ROWS, 1024))
        ab[k, 0:ROWS, :] = high
        ab[k, ROWS:, :] = low
        product_one(k, 0)
        push(tp.at[k, at_z(4), 0], zu1.at[k], k, RU, up)
        push(tp.at[k, at_z(4), 1], zd1.at[k], k, RD, down)

    def a4b(k):
        for step in (1, 2, 3):
            product_one(k, step)
        for slot, owner in enumerate((z_up, z_down, z)):
            remote(tp.at[k, owner, other], yo.at[k, slot], k, OWN, ypart).start()
        sent.append(remote(yo.at[k], yo.at[k], k, OWN, ypart))

    def z2(k):
        remote(zu1.at[k], zu1.at[k], k, RU, up).wait_recv()
        tp[k, at_z(3), 0] = tp[k, at_z(3), 0] + zu1[k]
        push(tp.at[k, at_z(3)], zu.at[k], k, RU + 1, up)
        remote(zd1.at[k], zd1.at[k], k, RD, down).wait_recv()
        tp[k, at_z(-3), 1] = tp[k, at_z(-3), 1] + zd1[k]
        push(tp.at[k, at_z(-3)], zd.at[k], k, RD + 1, down)

    def z3(k):
        remote(zu.at[k], zu.at[k], k, RU + 1, up).wait_recv()
        tp[k, at_z(2)] = tp[k, at_z(2)] + zu[k]
        remote(tp.at[k, at_z(2), other], zhu.at[k, 1], k, HALF_U, up_other).start()
        remote(tp.at[k, at_z(2), ylo], zhu.at[k, 0], k, HALF_U, up).start()
        sent.append(remote(zhu.at[k], zhu.at[k], k, HALF_U, up))
        remote(zd.at[k], zd.at[k], k, RD + 1, down).wait_recv()
        tp[k, at_z(-2)] = tp[k, at_z(-2)] + zd[k]
        remote(tp.at[k, at_z(-2), other], zhd.at[k, 1], k, HALF_D, down_other).start()
        remote(tp.at[k, at_z(-2), ylo], zhd.at[k, 0], k, HALF_D, down).start()
        sent.append(remote(zhd.at[k], zhd.at[k], k, HALF_D, down))

    def z4(k):
        remote(yo.at[k], yo.at[k], k, OWN, ypart).wait_recv()
        remote(zhu.at[k], zhu.at[k], k, HALF_U, up).wait_recv()
        tp[k, z_up, ylo] = tp[k, z_up, ylo] + (yo[k, 0] + (zhu[k, 0] + zhu[k, 1]))
        remote(tp.at[k, z_up, ylo], zl.at[k, 0], k, LAST, up).start()
        remote(zhd.at[k], zhd.at[k], k, HALF_D, down).wait_recv()
        tp[k, z_down, ylo] = tp[k, z_down, ylo] + (yo[k, 1] + (zhd[k, 0] + zhd[k, 1]))
        remote(tp.at[k, z_down, ylo], zl.at[k, 1], k, LAST, down).start()
        sent.append(remote(zl.at[k], zl.at[k], k, LAST, up))

    def z6(k):
        remote(zl.at[k], zl.at[k], k, LAST, up).wait_recv()
        tf[k, z, ylo] = tp[k, z, ylo] + (yo[k, 2] + (zl[k, 0] + zl[k, 1]))
        for device in (up, down, ypart):
            remote(tf.at[k, z, ylo], tf.at[k, z, ylo], k, FIRST, device).start()
        sent.append(remote(yo.at[k], yo.at[k], k, FIRST, up))

    def z7(k):
        remote(yo.at[k], yo.at[k], k, FIRST, up).wait_recv()
        below, above = tf.at[k, z_down, ylo], tf.at[k, z_up, ylo]
        remote(below, below, k, PASS_U, up_other).start()
        remote(below, below, k, PASS_U, up).start()
        remote(above, above, k, PASS_D, down_other).start()
        remote(above, above, k, PASS_D, down).start()
        remote(below, below, k, NEAR, ypart).start()
        remote(above, above, k, NEAR, ypart).start()
        for sem in (PASS_U, PASS_D, NEAR):
            sent.append(remote(zl.at[k], zl.at[k], k, sem, up))

    def z8(k):
        below, above = tf.at[k, at_z(-2)], tf.at[k, at_z(2)]
        remote(zl.at[k], zl.at[k], k, PASS_U, up).wait_recv()
        push(below, below, k, GU, up)
        remote(zl.at[k], zl.at[k], k, PASS_D, down).wait_recv()
        push(above, above, k, GD, down)

    def p1(k):
        remote(zl.at[k], zl.at[k], k, NEAR, ypart).wait_recv()
        product_two(k, 0)

    def z9(k):
        below, above = at_z(-3), at_z(3)
        remote(tf.at[k, below], tf.at[k, below], k, GU, up).wait_recv()
        push(tf.at[k, below, 0], tf.at[k, below, 0], k, GU + 1, up)
        remote(tf.at[k, above], tf.at[k, above], k, GD, down).wait_recv()
        push(tf.at[k, above, 1], tf.at[k, above, 1], k, GD + 1, down)

    def z11(k):
        far = at_z(4)
        remote(tf.at[k, far, 0], tf.at[k, far, 0], k, GU + 1, up).wait_recv()
        remote(tf.at[k, far, 1], tf.at[k, far, 1], k, GD + 1, down).wait_recv()
        product_two(k, 3)
        push(ob.at[k, 1 - core], oc.at[k], k, CORE_O, sib)

    def b1(k):
        remote(oc.at[k], oc.at[k], k, CORE_O, sib).wait_recv()
        ob[k, core] = ob[k, core] + oc[k]
        for d in range(1, CHIPS):
            remote(ob.at[k, core, lax.rem(chip + d, CHIPS)], orv.at[k, d - 1], k, DIR_O, peer(d)).start()
        sent.append(remote(orv.at[k], orv.at[k], k, DIR_O, sib))

    def b2(k):
        remote(orv.at[k], orv.at[k], k, DIR_O, sib).wait_recv()
        total = ob[k, core, chip]
        for d in range(CHIPS - 1):
            total = total + orv[k, d]
        out_ref[k] = total

    stages = {
        "A0": a0, "A1": a1, "A2": a2, "A3": a3, "A4": a4, "A4b": a4b, "Z2": z2, "Z3": z3, "Z4": z4, "Z6": z6,
        "Z7": z7, "P1": p1, "Z8": z8, "P2": lambda k: product_two(k, 1),
        "Z9": z9, "P3": lambda k: product_two(k, 2), "Z11": z11, "B1": b1, "B2": b2,
        "x_load": lambda k: x_load(), "h_prep": lambda k: h_prep(), "x_prep": lambda k: x_prep(),
    }
    for name, k in ORDER:
        stages[name](k)
    for copy in sent:
        copy.wait_send()


def on_device(x_matrix, h_matrix, x_mask, h_mask, panel):
    n, slab = x_matrix.shape[0], 32 // CHUNKS
    part = (ROWS // 2, EDGE)
    f32, bf16 = jnp.float32, jnp.bfloat16
    vmem, hbm = pl.BlockSpec(memory_space=pltpu.VMEM), pl.BlockSpec(memory_space=pl.ANY)
    out = pl.pallas_call(
        kernel,
        out_shape=jax.ShapeDtypeStruct((CHUNKS, slab, n), f32),
        in_specs=[hbm, hbm, vmem, vmem, pl.BlockSpec(memory_space=pltpu.SMEM)],
        out_specs=vmem,
        scratch_shapes=[
            pltpu.VMEM((2, CHIPS, 2, CHUNKS, slab, n), f32),
            pltpu.VMEM((n, n), f32),
            pltpu.VMEM((n, n), bf16), pltpu.VMEM((n, n), bf16),
            pltpu.VMEM((n, n), bf16), pltpu.VMEM((n, n), bf16),
            pltpu.VMEM((2, 4, n), f32), pltpu.VMEM((8, n), f32), pltpu.VMEM((8, n), f32),
            pltpu.VMEM((CHUNKS, 2, CHIPS, slab, n), f32),
            pltpu.VMEM((CHUNKS, CHIPS, slab, n), f32),
            pltpu.VMEM((CHUNKS, CHIPS - 1, slab, n), f32),
            pltpu.VMEM((CHUNKS, 2, CHIPS, slab, n), f32),
            pltpu.VMEM((CHUNKS, 2 * ROWS, n), bf16), pltpu.VMEM((2 * ROWS, 2 * EDGE), bf16),
            pltpu.VMEM((CHUNKS, RING, 2, *part), f32),
            pltpu.VMEM((CHUNKS, *part), f32), pltpu.VMEM((CHUNKS, *part), f32),
            pltpu.VMEM((CHUNKS, 2, *part), f32), pltpu.VMEM((CHUNKS, 2, *part), f32),
            pltpu.VMEM((CHUNKS, 2, *part), f32), pltpu.VMEM((CHUNKS, 2, *part), f32),
            pltpu.VMEM((CHUNKS, 2, *part), f32), pltpu.VMEM((CHUNKS, 3, *part), f32),
            pltpu.VMEM((CHUNKS, RING, 2, *part), f32),
            pltpu.VMEM((CHUNKS, 2, CHIPS, slab, n), f32),
            pltpu.VMEM((CHUNKS, CHIPS, slab, n), f32),
            pltpu.VMEM((CHUNKS, CHIPS - 1, slab, n), f32),
            pltpu.SemaphoreType.DMA((2,)),
            pltpu.SemaphoreType.DMA((CHUNKS, N_SEMS)),
            pltpu.SemaphoreType.DMA((CHUNKS, N_SEMS)),
        ],
        compiler_params=pltpu.CompilerParams(
            collective_id=0, has_side_effects=True, vmem_limit_bytes=56 * 1024 * 1024),
    )(x_matrix.reshape(2, CHIPS, 2, CHUNKS, slab, n), h_matrix, x_mask, h_mask, panel)
    return out.reshape(32, n)


def solution(mesh):
    return jax.shard_map(
        on_device,
        mesh=mesh,
        in_specs=(P("row", "col"), P("row", "col"), P("row", "col"), P("row", "col"), P()),
        out_specs=P("row", "col"),
        check_vma=False,
    )
```

```python
import functools

import jax
import jax.numpy as jnp
from jax import lax
from jax.experimental import pallas as pl
from jax.experimental.pallas import tpu as pltpu
from jax.sharding import PartitionSpec as P

MESH = pl.DeviceIdType.MESH
CHUNKS = 4
PANEL = 512
ROWS = PANEL // CHUNKS
CHIPS = 8
RING = 8
EDGE = 128

ORDER = (
    ("x_load", 0), ("A0", 3), ("A1", 3), ("A0", 0), ("A1", 0), ("A0", 2), ("A1", 2), ("A2", 3), ("h_prep", 0),
    ("A2", 0), ("A0", 1), ("A1", 1), ("x_prep", 0), ("A3", 3), ("A4", 3), ("A2", 2), ("A3", 0), ("A4b", 3),
    ("A4", 0), ("Z2", 3), ("A2", 1), ("A4b", 0), ("Z2", 0), ("A3", 2), ("A4", 2), ("Z3", 3), ("A3", 1), ("Z3", 0),
    ("A4b", 2), ("A4", 1), ("Z2", 2), ("A4b", 1), ("Z4", 3), ("Z4", 0), ("Z2", 1), ("Z3", 2), ("Z6", 3),
    ("Z6", 0), ("Z3", 1), ("Z4", 2), ("Z7", 3), ("Z4", 1), ("Z6", 2), ("Z7", 0), ("Z8", 3), ("Z6", 1), ("Z7", 2),
    ("Z8", 0), ("P1", 3), ("Z9", 3), ("Z7", 1), ("Z8", 2), ("P1", 2), ("P1", 0), ("Z9", 0), ("P2", 3), ("P3", 3),
    ("Z11", 3), ("P2", 0), ("P3", 0), ("Z8", 1), ("B1", 3), ("Z9", 2), ("P2", 2), ("P3", 2), ("Z11", 0),
    ("B1", 0), ("P1", 1), ("Z9", 1), ("Z11", 2), ("B1", 2), ("P2", 1), ("P3", 1), ("Z11", 1), ("B1", 1),
    ("B2", 2), ("B2", 3), ("B2", 0), ("B2", 1),
)

CORE_P, DIR_P, AG_P, CORE_R, CORE_O, DIR_O, OWN, HALF_U, HALF_D, LAST, FIRST, NEAR, PASS_U, PASS_D = range(14)
RU, RD, GU, GD = 14, 16, 18, 20
N_SEMS = 22


def kernel(x_hbm, h_hbm, xm_hbm, hm_hbm, panel_ref, out_ref,
           xm_ref, hm_ref, xv, hv, xh, xl, hh, hl, wx, mx, mh, piece, pc, pr, rr, ab, tb, tp, zu1, zd1, zu, zd, zhu, zhd, zl, yo, tf,
           ob, oc, orv, load_sem, send, recv):
    row, col = lax.axis_index("row"), lax.axis_index("col")
    core, chip = lax.rem(row, 2), lax.div(row, 2)
    z, ylo = lax.rem(col, RING), lax.div(col, RING)
    sib = (row + 1 - 2 * core, col)
    other = 1 - ylo
    ypart = (row, other * RING + z)
    z_up, z_down = lax.rem(z + 1, RING), lax.rem(z + RING - 1, RING)
    up, up_other = (row, ylo * RING + z_up), (row, other * RING + z_up)
    down, down_other = (row, ylo * RING + z_down), (row, other * RING + z_down)
    around = [up, down, up_other, down_other, ypart]

    def peer(d):
        return (lax.rem(chip + d, CHIPS) * 2 + core, col)

    def at_z(d):
        return lax.rem(z + (d + RING) % RING, RING)

    load_x = pltpu.make_async_copy(x_hbm, xv, load_sem.at[0])
    load_h = pltpu.make_async_copy(h_hbm, hv, load_sem.at[1])
    load_xm = pltpu.make_async_copy(xm_hbm, xm_ref, load_sem.at[2])
    load_hm = pltpu.make_async_copy(hm_hbm, hm_ref, load_sem.at[3])
    load_xm.start()
    load_x.start()
    load_hm.start()

    barrier = pltpu.get_barrier_semaphore()
    friends = [sib] + around + [peer(d) for d in range(1, CHIPS)]
    for friend in friends:
        pl.semaphore_signal(barrier, inc=1, device_id=friend, device_id_type=MESH)

    def remote(src, dst, k, sem, device):
        return pltpu.make_async_remote_copy(
            src_ref=src, dst_ref=dst, send_sem=send.at[k, sem], recv_sem=recv.at[k, sem],
            device_id=device, device_id_type=MESH)

    sent = []

    def push(src, dst, k, sem, device):
        copy = remote(src, dst, k, sem, device)
        copy.start()
        sent.append(copy)

    def spread(mask):
        m = mask.astype(jnp.float32)
        return jnp.concatenate(
            [jnp.broadcast_to(m[:, j:j + 1], (m.shape[0], EDGE)) for j in range(m.shape[1])], axis=1)

    def split(value):
        high = value.astype(jnp.bfloat16)
        return high, (value - high.astype(jnp.float32)).astype(jnp.bfloat16)

    def product_one(k, step):
        far = lax.div(at_z(4), 2)
        turn = 1 - 2 * lax.rem(z + 1, 2)
        pair = lax.rem(far + (0, 4 + turn, 4 - turn, 2)[step], 4)
        rows = pl.ds(pl.multiple_of(pair * 256, 256), 256)
        dims = (((1,), (1,)), ((), ()))
        first = lax.dot_general(ab[k], hh[rows, :], dims, preferred_element_type=jnp.float32)
        second = lax.dot_general(ab[k, 0:ROWS, :], hl[rows, :], dims, preferred_element_type=jnp.float32)
        value = first[:ROWS] + (first[ROWS:] + second)
        tp[k, 2 * pair] = value[:, :EDGE].reshape(2, ROWS // 2, EDGE)
        tp[k, 2 * pair + 1] = value[:, EDGE:].reshape(2, ROWS // 2, EDGE)

    def product_two(k, step):
        turn = 1 - 2 * lax.rem(z + 1, 2)
        pair = lax.rem(lax.div(z, 2) + (0, 4 + turn, 4 - turn, 2)[step], 4)
        for half in range(2):
            a, b = split(tf[k, 2 * pair + half].reshape(ROWS, EDGE))
            tb[0:ROWS, half * EDGE:(half + 1) * EDGE] = a
            tb[ROWS:, half * EDGE:(half + 1) * EDGE] = b
        rows = pl.ds(pl.multiple_of(pair * 256, 256), 256)
        for n in range(0, 1024, 256):
            first = jnp.dot(tb[...], xh[rows, n:n + 256], preferred_element_type=jnp.float32)
            second = jnp.dot(tb[0:ROWS, :], xl[rows, n:n + 256], preferred_element_type=jnp.float32)
            value = (first[:ROWS] + (first[ROWS:] + second)).reshape(2, CHIPS, ROWS // 16, 256)
            ob[k, :, :, :, n:n + 256] = value if step == 0 else ob[k, :, :, :, n:n + 256] + value

    def x_load():
        load_xm.wait()
        mx[...] = spread(xm_ref[...])
        s0 = jnp.where(panel_ref[0] == 2 * row, 1.0, 0.0)
        s1 = jnp.where(panel_ref[0] == 2 * row + 1, 1.0, 0.0)
        wx[0] = mx[0:4, :] * s0
        wx[1] = mx[4:8, :] * s1
        load_x.wait()
        load_h.start()

    def h_prep():
        load_hm.wait()
        mh[...] = spread(hm_ref[...])
        load_h.wait()

        def body(b, carry):
            rows = pl.ds(pl.multiple_of(b * EDGE, EDGE), EDGE)
            high, low = split(hv[rows, :] * mh[pl.ds(b, 1), :])
            hh[rows, :] = high
            hl[rows, :] = low
            return carry

        lax.fori_loop(0, 8, body, 0)

    def x_prep():
        def body(b, carry):
            rows = pl.ds(pl.multiple_of(b * EDGE, EDGE), EDGE)
            block = xv[lax.div(b, 4), pl.ds(lax.rem(b, 4) * 2, 2)].reshape(EDGE, 1024)
            high, low = split(block * mx[pl.ds(b, 1), :])
            xh[rows, :] = high
            xl[rows, :] = low
            return carry

        lax.fori_loop(0, 8, body, 0)

    def a0(k):
        for q in range(2):
            for g in range(CHIPS):
                w0, w1 = wx[0, g // 2:g // 2 + 1, :], wx[1, g // 2:g // 2 + 1, :]
                piece[k, q, g] = xv[0, g, q, k] * w0 + xv[1, g, q, k] * w1
        if not sent:
            pl.semaphore_wait(barrier, len(friends))
        push(piece.at[k, 1 - core], pc.at[k], k, CORE_P, sib)

    def a1(k):
        remote(pc.at[k], pc.at[k], k, CORE_P, sib).wait_recv()
        piece[k, core] = piece[k, core] + pc[k]
        for d in range(1, CHIPS):
            remote(piece.at[k, core, lax.rem(chip + d, CHIPS)], pr.at[k, d - 1], k, DIR_P, peer(d)).start()
        sent.append(remote(pr.at[k], pr.at[k], k, DIR_P, sib))

    def a2(k):
        remote(pr.at[k], pr.at[k], k, DIR_P, sib).wait_recv()
        total = piece[k, core, chip]
        for d in range(CHIPS - 1):
            total = total + pr[k, d]
        rr[k, core, chip] = total
        for d in range(1, CHIPS):
            remote(rr.at[k, core, chip], rr.at[k, core, chip], k, AG_P, peer(d)).start()
        sent.append(remote(pr.at[k], pr.at[k], k, AG_P, sib))

    def a3(k):
        remote(pr.at[k], pr.at[k], k, AG_P, sib).wait_recv()
        push(rr.at[k, core], rr.at[k, core], k, CORE_R, sib)

    def a4(k):
        remote(rr.at[k, core], rr.at[k, 1 - core], k, CORE_R, sib).wait_recv()
        high, low = split(rr[k].reshape(ROWS, 1024))
        ab[k, 0:ROWS, :] = high
        ab[k, ROWS:, :] = low
        product_one(k, 0)
        push(tp.at[k, at_z(4), 0], zu1.at[k], k, RU, up)
        push(tp.at[k, at_z(4), 1], zd1.at[k], k, RD, down)

    def a4b(k):
        for step in (1, 2, 3):
            product_one(k, step)
        for slot, owner in enumerate((z_up, z_down, z)):
            remote(tp.at[k, owner, other], yo.at[k, slot], k, OWN, ypart).start()
        sent.append(remote(yo.at[k], yo.at[k], k, OWN, ypart))

    def z2(k):
        remote(zu1.at[k], zu1.at[k], k, RU, up).wait_recv()
        tp[k, at_z(3), 0] = tp[k, at_z(3), 0] + zu1[k]
        push(tp.at[k, at_z(3)], zu.at[k], k, RU + 1, up)
        remote(zd1.at[k], zd1.at[k], k, RD, down).wait_recv()
        tp[k, at_z(-3), 1] = tp[k, at_z(-3), 1] + zd1[k]
        push(tp.at[k, at_z(-3)], zd.at[k], k, RD + 1, down)

    def z3(k):
        remote(zu.at[k], zu.at[k], k, RU + 1, up).wait_recv()
        tp[k, at_z(2)] = tp[k, at_z(2)] + zu[k]
        remote(tp.at[k, at_z(2), other], zhu.at[k, 1], k, HALF_U, up_other).start()
        remote(tp.at[k, at_z(2), ylo], zhu.at[k, 0], k, HALF_U, up).start()
        sent.append(remote(zhu.at[k], zhu.at[k], k, HALF_U, up))
        remote(zd.at[k], zd.at[k], k, RD + 1, down).wait_recv()
        tp[k, at_z(-2)] = tp[k, at_z(-2)] + zd[k]
        remote(tp.at[k, at_z(-2), other], zhd.at[k, 1], k, HALF_D, down_other).start()
        remote(tp.at[k, at_z(-2), ylo], zhd.at[k, 0], k, HALF_D, down).start()
        sent.append(remote(zhd.at[k], zhd.at[k], k, HALF_D, down))

    def z4(k):
        remote(yo.at[k], yo.at[k], k, OWN, ypart).wait_recv()
        remote(zhu.at[k], zhu.at[k], k, HALF_U, up).wait_recv()
        tp[k, z_up, ylo] = tp[k, z_up, ylo] + (yo[k, 0] + (zhu[k, 0] + zhu[k, 1]))
        remote(tp.at[k, z_up, ylo], zl.at[k, 0], k, LAST, up).start()
        remote(zhd.at[k], zhd.at[k], k, HALF_D, down).wait_recv()
        tp[k, z_down, ylo] = tp[k, z_down, ylo] + (yo[k, 1] + (zhd[k, 0] + zhd[k, 1]))
        remote(tp.at[k, z_down, ylo], zl.at[k, 1], k, LAST, down).start()
        sent.append(remote(zl.at[k], zl.at[k], k, LAST, up))

    def z6(k):
        remote(zl.at[k], zl.at[k], k, LAST, up).wait_recv()
        tf[k, z, ylo] = tp[k, z, ylo] + (yo[k, 2] + (zl[k, 0] + zl[k, 1]))
        for device in (up, down, ypart):
            remote(tf.at[k, z, ylo], tf.at[k, z, ylo], k, FIRST, device).start()
        sent.append(remote(yo.at[k], yo.at[k], k, FIRST, up))

    def z7(k):
        remote(yo.at[k], yo.at[k], k, FIRST, up).wait_recv()
        below, above = tf.at[k, z_down, ylo], tf.at[k, z_up, ylo]
        remote(below, below, k, PASS_U, up_other).start()
        remote(below, below, k, PASS_U, up).start()
        remote(above, above, k, PASS_D, down_other).start()
        remote(above, above, k, PASS_D, down).start()
        remote(below, below, k, NEAR, ypart).start()
        remote(above, above, k, NEAR, ypart).start()
        for sem in (PASS_U, PASS_D, NEAR):
            sent.append(remote(zl.at[k], zl.at[k], k, sem, up))

    def z8(k):
        below, above = tf.at[k, at_z(-2)], tf.at[k, at_z(2)]
        remote(zl.at[k], zl.at[k], k, PASS_U, up).wait_recv()
        push(below, below, k, GU, up)
        remote(zl.at[k], zl.at[k], k, PASS_D, down).wait_recv()
        push(above, above, k, GD, down)

    def p1(k):
        remote(zl.at[k], zl.at[k], k, NEAR, ypart).wait_recv()
        product_two(k, 0)

    def z9(k):
        below, above = at_z(-3), at_z(3)
        remote(tf.at[k, below], tf.at[k, below], k, GU, up).wait_recv()
        push(tf.at[k, below, 0], tf.at[k, below, 0], k, GU + 1, up)
        remote(tf.at[k, above], tf.at[k, above], k, GD, down).wait_recv()
        push(tf.at[k, above, 1], tf.at[k, above, 1], k, GD + 1, down)

    def z11(k):
        far = at_z(4)
        remote(tf.at[k, far, 0], tf.at[k, far, 0], k, GU + 1, up).wait_recv()
        remote(tf.at[k, far, 1], tf.at[k, far, 1], k, GD + 1, down).wait_recv()
        product_two(k, 3)
        push(ob.at[k, 1 - core], oc.at[k], k, CORE_O, sib)

    def b1(k):
        remote(oc.at[k], oc.at[k], k, CORE_O, sib).wait_recv()
        ob[k, core] = ob[k, core] + oc[k]
        for d in range(1, CHIPS):
            remote(ob.at[k, core, lax.rem(chip + d, CHIPS)], orv.at[k, d - 1], k, DIR_O, peer(d)).start()
        sent.append(remote(orv.at[k], orv.at[k], k, DIR_O, sib))

    def b2(k):
        remote(orv.at[k], orv.at[k], k, DIR_O, sib).wait_recv()
        total = ob[k, core, chip]
        for d in range(CHIPS - 1):
            total = total + orv[k, d]
        out_ref[k] = total

    stages = {
        "A0": a0, "A1": a1, "A2": a2, "A3": a3, "A4": a4, "A4b": a4b, "Z2": z2, "Z3": z3, "Z4": z4, "Z6": z6,
        "Z7": z7, "P1": p1, "Z8": z8, "P2": lambda k: product_two(k, 1),
        "Z9": z9, "P3": lambda k: product_two(k, 2), "Z11": z11, "B1": b1, "B2": b2,
        "x_load": lambda k: x_load(), "h_prep": lambda k: h_prep(), "x_prep": lambda k: x_prep(),
    }
    for name, k in ORDER:
        stages[name](k)
    for copy in sent:
        copy.wait_send()


def on_device(x_matrix, h_matrix, x_mask, h_mask, panel):
    n, slab = x_matrix.shape[0], 32 // CHUNKS
    part = (ROWS // 2, EDGE)
    f32, bf16 = jnp.float32, jnp.bfloat16
    vmem, hbm = pl.BlockSpec(memory_space=pltpu.VMEM), pl.BlockSpec(memory_space=pl.ANY)
    out = pl.pallas_call(
        kernel,
        out_shape=pltpu.VMEM((CHUNKS, slab, n), f32),
        in_specs=[hbm, hbm, hbm, hbm, pl.BlockSpec(memory_space=pltpu.SMEM)],
        out_specs=vmem,
        scratch_shapes=[
            pltpu.VMEM((8, 8), jnp.int32), pltpu.VMEM((8, 8), jnp.int32),
            pltpu.VMEM((2, CHIPS, 2, CHUNKS, slab, n), f32),
            pltpu.VMEM((n, n), f32),
            pltpu.VMEM((n, n), bf16), pltpu.VMEM((n, n), bf16),
            pltpu.VMEM((n, n), bf16), pltpu.VMEM((n, n), bf16),
            pltpu.VMEM((2, 4, n), f32), pltpu.VMEM((8, n), f32), pltpu.VMEM((8, n), f32),
            pltpu.VMEM((CHUNKS, 2, CHIPS, slab, n), f32),
            pltpu.VMEM((CHUNKS, CHIPS, slab, n), f32),
            pltpu.VMEM((CHUNKS, CHIPS - 1, slab, n), f32),
            pltpu.VMEM((CHUNKS, 2, CHIPS, slab, n), f32),
            pltpu.VMEM((CHUNKS, 2 * ROWS, n), bf16), pltpu.VMEM((2 * ROWS, 2 * EDGE), bf16),
            pltpu.VMEM((CHUNKS, RING, 2, *part), f32),
            pltpu.VMEM((CHUNKS, *part), f32), pltpu.VMEM((CHUNKS, *part), f32),
            pltpu.VMEM((CHUNKS, 2, *part), f32), pltpu.VMEM((CHUNKS, 2, *part), f32),
            pltpu.VMEM((CHUNKS, 2, *part), f32), pltpu.VMEM((CHUNKS, 2, *part), f32),
            pltpu.VMEM((CHUNKS, 2, *part), f32), pltpu.VMEM((CHUNKS, 3, *part), f32),
            pltpu.VMEM((CHUNKS, RING, 2, *part), f32),
            pltpu.VMEM((CHUNKS, 2, CHIPS, slab, n), f32),
            pltpu.VMEM((CHUNKS, CHIPS, slab, n), f32),
            pltpu.VMEM((CHUNKS, CHIPS - 1, slab, n), f32),
            pltpu.SemaphoreType.DMA((4,)),
            pltpu.SemaphoreType.DMA((CHUNKS, N_SEMS)),
            pltpu.SemaphoreType.DMA((CHUNKS, N_SEMS)),
        ],
        compiler_params=pltpu.CompilerParams(
            collective_id=0, has_side_effects=True, vmem_limit_bytes=56 * 1024 * 1024),
    )(x_matrix.reshape(2, CHIPS, 2, CHUNKS, slab, n), h_matrix, x_mask, h_mask, panel)
    return out.reshape(32, n)


def solution(mesh):
    return jax.shard_map(
        on_device,
        mesh=mesh,
        in_specs=(P("row", "col"), P("row", "col"), P("row", "col"), P("row", "col"), P()),
        out_specs=P("row", "col"),
        check_vma=False,
    )
```

```python
import functools

import jax
import jax.numpy as jnp
from jax import lax
from jax.experimental import pallas as pl
from jax.experimental.pallas import tpu as pltpu
from jax.sharding import PartitionSpec as P

MESH = pl.DeviceIdType.MESH
CHUNKS = 4
PANEL = 512
ROWS = PANEL // CHUNKS
CHIPS = 8
RING = 8
EDGE = 128

SHORT_SUM = (0, 1, 2, 3)
SHORT_GATHER = (0, 1, 2, 3)

ORDER = (
    ("x_load", 0), ("A0", 0), ("A1", 0), ("A0", 2), ("A1", 2), ("A0", 1), ("A0", 3), ("A1", 1), ("A2", 0),
    ("h_prep", 0), ("A2", 2), ("A1", 3), ("A3", 0), ("A2", 1), ("A4", 0), ("A4b", 0), ("A3", 2), ("A4", 2),
    ("A2", 3), ("A3", 1), ("Z3", 0), ("A4", 1), ("A4b", 2), ("Z3", 2), ("A4b", 1), ("A3", 3), ("Z4", 0),
    ("A4", 3), ("A4b", 3), ("Z3", 1), ("Z4", 2), ("Z6", 0), ("x_prep", 0), ("Z3", 3), ("Z4", 1), ("Z6", 2),
    ("Z7", 0), ("Z4", 3), ("Z6", 1), ("Z7", 2), ("Z8", 0), ("Z6", 3), ("Z7", 1), ("Z8", 2), ("P1", 0), ("Z7", 3),
    ("P1", 2), ("P2", 0), ("Z11", 0), ("Z8", 1), ("P1", 1), ("P2", 2), ("B1", 0), ("Z11", 2), ("Z8", 3),
    ("P1", 3), ("P2", 3), ("B1", 2), ("P2", 1), ("Z11", 1), ("B1", 1), ("B2", 0), ("Z11", 3), ("B1", 3),
    ("B2", 1), ("B2", 2), ("B2", 3),
)

CORE_P, DIR_P, AG_P, CORE_R, CORE_O, DIR_O, OWN, HALF_U, HALF_D, LAST, FIRST, NEAR, PASS_U, PASS_D = range(14)
RU, RD, GU, GD = 14, 16, 18, 20
N_SEMS = 22


def kernel(x_hbm, h_hbm, xm_hbm, hm_hbm, panel_ref, out_ref,
           xm_ref, hm_ref, xv, hv, xh, xl, hh, hl, wx, mx, mh, piece, pc, pr, rr, ab, tb, tp, zu1, zd1, zu, zd, zhu, zhd, zl, yo, tf,
           ob, oc, orv, load_sem, send, recv):
    row, col = lax.axis_index("row"), lax.axis_index("col")
    core, chip = lax.rem(row, 2), lax.div(row, 2)
    z, ylo = lax.rem(col, RING), lax.div(col, RING)
    sib = (row + 1 - 2 * core, col)
    def at_z(d):
        return lax.rem(z + (d + RING) % RING, RING)

    other = 1 - ylo
    ypart = (row, other * RING + z)
    z_up, z_down = lax.rem(z + 1, RING), lax.rem(z + RING - 1, RING)
    up, up_other = (row, ylo * RING + z_up), (row, other * RING + z_up)
    down, down_other = (row, ylo * RING + z_down), (row, other * RING + z_down)
    up_two, down_two = (row, ylo * RING + at_z(2)), (row, ylo * RING + at_z(-2))
    around = [up_two, down_two, up, down, up_other, down_other, ypart]

    def peer(d):
        return (lax.rem(chip + d, CHIPS) * 2 + core, col)

    load_x = pltpu.make_async_copy(x_hbm, xv, load_sem.at[0])
    load_h = pltpu.make_async_copy(h_hbm, hv, load_sem.at[1])
    load_xm = pltpu.make_async_copy(xm_hbm, xm_ref, load_sem.at[2])
    load_hm = pltpu.make_async_copy(hm_hbm, hm_ref, load_sem.at[3])
    load_xm.start()
    load_x.start()
    load_hm.start()

    barrier = pltpu.get_barrier_semaphore()
    friends = [sib] + around + [peer(d) for d in range(1, CHIPS)]
    for friend in friends:
        pl.semaphore_signal(barrier, inc=1, device_id=friend, device_id_type=MESH)

    def remote(src, dst, k, sem, device):
        return pltpu.make_async_remote_copy(
            src_ref=src, dst_ref=dst, send_sem=send.at[k, sem], recv_sem=recv.at[k, sem],
            device_id=device, device_id_type=MESH)

    sent = []

    def push(src, dst, k, sem, device):
        copy = remote(src, dst, k, sem, device)
        copy.start()
        sent.append(copy)

    def spread(mask):
        m = mask.astype(jnp.float32)
        return jnp.concatenate(
            [jnp.broadcast_to(m[:, j:j + 1], (m.shape[0], EDGE)) for j in range(m.shape[1])], axis=1)

    def split(value):
        high = value.astype(jnp.bfloat16)
        return high, (value - high.astype(jnp.float32)).astype(jnp.bfloat16)

    def product_one(k, step):
        far = lax.div(at_z(4), 2)
        turn = 1 - 2 * lax.rem(z + 1, 2)
        pair = lax.rem(far + (0, 4 + turn, 4 - turn, 2)[step], 4)
        rows = pl.ds(pl.multiple_of(pair * 256, 256), 256)
        dims = (((1,), (1,)), ((), ()))
        first = lax.dot_general(ab[k], hh[rows, :], dims, preferred_element_type=jnp.float32)
        second = lax.dot_general(ab[k, 0:ROWS, :], hl[rows, :], dims, preferred_element_type=jnp.float32)
        value = first[:ROWS] + (first[ROWS:] + second)
        tp[k, 2 * pair] = value[:, :EDGE].reshape(2, ROWS // 2, EDGE)
        tp[k, 2 * pair + 1] = value[:, EDGE:].reshape(2, ROWS // 2, EDGE)

    def product_two(k, step):
        turn = 1 - 2 * lax.rem(z + 1, 2)
        pair = lax.rem(lax.div(z, 2) + (0, 4 + turn, 4 - turn, 2)[step], 4)
        for half in range(2):
            a, b = split(tf[k, 2 * pair + half].reshape(ROWS, EDGE))
            tb[0:ROWS, half * EDGE:(half + 1) * EDGE] = a
            tb[ROWS:, half * EDGE:(half + 1) * EDGE] = b
        rows = pl.ds(pl.multiple_of(pair * 256, 256), 256)
        for n in range(0, 1024, 256):
            first = jnp.dot(tb[...], xh[rows, n:n + 256], preferred_element_type=jnp.float32)
            second = jnp.dot(tb[0:ROWS, :], xl[rows, n:n + 256], preferred_element_type=jnp.float32)
            value = (first[:ROWS] + (first[ROWS:] + second)).reshape(2, CHIPS, ROWS // 16, 256)
            ob[k, :, :, :, n:n + 256] = value if step == 0 else ob[k, :, :, :, n:n + 256] + value

    def x_load():
        load_xm.wait()
        mx[...] = spread(xm_ref[...])
        s0 = jnp.where(panel_ref[0] == 2 * row, 1.0, 0.0)
        s1 = jnp.where(panel_ref[0] == 2 * row + 1, 1.0, 0.0)
        wx[0] = mx[0:4, :] * s0
        wx[1] = mx[4:8, :] * s1
        load_x.wait()
        load_h.start()

    def h_prep():
        load_hm.wait()
        mh[...] = spread(hm_ref[...])
        load_h.wait()

        def body(b, carry):
            rows = pl.ds(pl.multiple_of(b * EDGE, EDGE), EDGE)
            high, low = split(hv[rows, :] * mh[pl.ds(b, 1), :])
            hh[rows, :] = high
            hl[rows, :] = low
            return carry

        lax.fori_loop(0, 8, body, 0)

    def x_prep():
        def body(b, carry):
            rows = pl.ds(pl.multiple_of(b * EDGE, EDGE), EDGE)
            block = xv[lax.div(b, 4), pl.ds(lax.rem(b, 4) * 2, 2)].reshape(EDGE, 1024)
            high, low = split(block * mx[pl.ds(b, 1), :])
            xh[rows, :] = high
            xl[rows, :] = low
            return carry

        lax.fori_loop(0, 8, body, 0)

    def a0(k):
        for q in range(2):
            for g in range(CHIPS):
                w0, w1 = wx[0, g // 2:g // 2 + 1, :], wx[1, g // 2:g // 2 + 1, :]
                piece[k, q, g] = xv[0, g, q, k] * w0 + xv[1, g, q, k] * w1
        if not sent:
            pl.semaphore_wait(barrier, len(friends))
        push(piece.at[k, 1 - core], pc.at[k], k, CORE_P, sib)

    def a1(k):
        remote(pc.at[k], pc.at[k], k, CORE_P, sib).wait_recv()
        piece[k, core] = piece[k, core] + pc[k]
        for d in range(1, CHIPS):
            remote(piece.at[k, core, lax.rem(chip + d, CHIPS)], pr.at[k, d - 1], k, DIR_P, peer(d)).start()
        sent.append(remote(pr.at[k], pr.at[k], k, DIR_P, sib))

    def a2(k):
        remote(pr.at[k], pr.at[k], k, DIR_P, sib).wait_recv()
        total = piece[k, core, chip]
        for d in range(CHIPS - 1):
            total = total + pr[k, d]
        rr[k, core, chip] = total
        for d in range(1, CHIPS):
            remote(rr.at[k, core, chip], rr.at[k, core, chip], k, AG_P, peer(d)).start()
        sent.append(remote(pr.at[k], pr.at[k], k, AG_P, sib))

    def a3(k):
        remote(pr.at[k], pr.at[k], k, AG_P, sib).wait_recv()
        push(rr.at[k, core], rr.at[k, core], k, CORE_R, sib)

    def a4(k):
        remote(rr.at[k, core], rr.at[k, 1 - core], k, CORE_R, sib).wait_recv()
        high, low = split(rr[k].reshape(ROWS, 1024))
        ab[k, 0:ROWS, :] = high
        ab[k, ROWS:, :] = low
        product_one(k, 0)
        if k in SHORT_SUM:
            product_one(k, 1)
            push(tp.at[k, at_z(4), 0], zu1.at[k], k, RU, up_two)
            push(tp.at[k, at_z(4), 1], zd1.at[k], k, RD, down_two)
            push(tp.at[k, at_z(3)], zu.at[k], k, RU + 1, up)
            push(tp.at[k, at_z(-3)], zd.at[k], k, RD + 1, down)
        else:
            push(tp.at[k, at_z(4), 0], zu1.at[k], k, RU, up)
            push(tp.at[k, at_z(4), 1], zd1.at[k], k, RD, down)

    def a4b(k):
        for step in (2, 3) if k in SHORT_SUM else (1, 2, 3):
            product_one(k, step)
        for slot, owner in enumerate((z_up, z_down, z)):
            remote(tp.at[k, owner, other], yo.at[k, slot], k, OWN, ypart).start()
        sent.append(remote(yo.at[k], yo.at[k], k, OWN, ypart))

    def z2(k):
        remote(zu1.at[k], zu1.at[k], k, RU, up).wait_recv()
        tp[k, at_z(3), 0] = tp[k, at_z(3), 0] + zu1[k]
        push(tp.at[k, at_z(3)], zu.at[k], k, RU + 1, up)
        remote(zd1.at[k], zd1.at[k], k, RD, down).wait_recv()
        tp[k, at_z(-3), 1] = tp[k, at_z(-3), 1] + zd1[k]
        push(tp.at[k, at_z(-3)], zd.at[k], k, RD + 1, down)

    def z3(k):
        if k in SHORT_SUM:
            remote(zu1.at[k], zu1.at[k], k, RU, up).wait_recv()
            tp[k, at_z(2), 0] = tp[k, at_z(2), 0] + zu1[k]
            remote(zd1.at[k], zd1.at[k], k, RD, down).wait_recv()
            tp[k, at_z(-2), 1] = tp[k, at_z(-2), 1] + zd1[k]
        remote(zu.at[k], zu.at[k], k, RU + 1, up).wait_recv()
        tp[k, at_z(2)] = tp[k, at_z(2)] + zu[k]
        remote(tp.at[k, at_z(2), other], zhu.at[k, 1], k, HALF_U, up_other).start()
        remote(tp.at[k, at_z(2), ylo], zhu.at[k, 0], k, HALF_U, up).start()
        sent.append(remote(zhu.at[k], zhu.at[k], k, HALF_U, up))
        remote(zd.at[k], zd.at[k], k, RD + 1, down).wait_recv()
        tp[k, at_z(-2)] = tp[k, at_z(-2)] + zd[k]
        remote(tp.at[k, at_z(-2), other], zhd.at[k, 1], k, HALF_D, down_other).start()
        remote(tp.at[k, at_z(-2), ylo], zhd.at[k, 0], k, HALF_D, down).start()
        sent.append(remote(zhd.at[k], zhd.at[k], k, HALF_D, down))

    def z4(k):
        remote(yo.at[k], yo.at[k], k, OWN, ypart).wait_recv()
        remote(zhu.at[k], zhu.at[k], k, HALF_U, up).wait_recv()
        tp[k, z_up, ylo] = tp[k, z_up, ylo] + (yo[k, 0] + (zhu[k, 0] + zhu[k, 1]))
        remote(tp.at[k, z_up, ylo], zl.at[k, 0], k, LAST, up).start()
        remote(zhd.at[k], zhd.at[k], k, HALF_D, down).wait_recv()
        tp[k, z_down, ylo] = tp[k, z_down, ylo] + (yo[k, 1] + (zhd[k, 0] + zhd[k, 1]))
        remote(tp.at[k, z_down, ylo], zl.at[k, 1], k, LAST, down).start()
        sent.append(remote(zl.at[k], zl.at[k], k, LAST, up))

    def z6(k):
        remote(zl.at[k], zl.at[k], k, LAST, up).wait_recv()
        tf[k, z, ylo] = tp[k, z, ylo] + (yo[k, 2] + (zl[k, 0] + zl[k, 1]))
        for device in (up, down, ypart):
            remote(tf.at[k, z, ylo], tf.at[k, z, ylo], k, FIRST, device).start()
        sent.append(remote(yo.at[k], yo.at[k], k, FIRST, up))

    def z7(k):
        remote(yo.at[k], yo.at[k], k, FIRST, up).wait_recv()
        below, above = tf.at[k, z_down, ylo], tf.at[k, z_up, ylo]
        remote(below, below, k, PASS_U, up_other).start()
        remote(below, below, k, PASS_U, up).start()
        remote(above, above, k, PASS_D, down_other).start()
        remote(above, above, k, PASS_D, down).start()
        remote(below, below, k, NEAR, ypart).start()
        remote(above, above, k, NEAR, ypart).start()
        for sem in (PASS_U, PASS_D, NEAR):
            sent.append(remote(zl.at[k], zl.at[k], k, sem, up))

    def z8(k):
        below, above = tf.at[k, at_z(-2)], tf.at[k, at_z(2)]
        remote(zl.at[k], zl.at[k], k, PASS_U, up).wait_recv()
        if k in SHORT_GATHER:
            push(below.at[0], below.at[0], k, GU + 1, up_two)
        push(below, below, k, GU, up)
        remote(zl.at[k], zl.at[k], k, PASS_D, down).wait_recv()
        if k in SHORT_GATHER:
            push(above.at[1], above.at[1], k, GD + 1, down_two)
        push(above, above, k, GD, down)

    def p1(k):
        remote(zl.at[k], zl.at[k], k, NEAR, ypart).wait_recv()
        product_two(k, 0)

    def z9(k):
        below, above = at_z(-3), at_z(3)
        remote(tf.at[k, below], tf.at[k, below], k, GU, up).wait_recv()
        push(tf.at[k, below, 0], tf.at[k, below, 0], k, GU + 1, up)
        remote(tf.at[k, above], tf.at[k, above], k, GD, down).wait_recv()
        push(tf.at[k, above, 1], tf.at[k, above, 1], k, GD + 1, down)

    def z11(k):
        far = at_z(4)
        remote(tf.at[k, far, 0], tf.at[k, far, 0], k, GU + 1, up).wait_recv()
        remote(tf.at[k, far, 1], tf.at[k, far, 1], k, GD + 1, down).wait_recv()
        if k in SHORT_GATHER:
            below, above = at_z(-3), at_z(3)
            remote(tf.at[k, below], tf.at[k, below], k, GU, up).wait_recv()
            remote(tf.at[k, above], tf.at[k, above], k, GD, down).wait_recv()
            product_two(k, 2)
        product_two(k, 3)
        push(ob.at[k, 1 - core], oc.at[k], k, CORE_O, sib)

    def b1(k):
        remote(oc.at[k], oc.at[k], k, CORE_O, sib).wait_recv()
        ob[k, core] = ob[k, core] + oc[k]
        for d in range(1, CHIPS):
            remote(ob.at[k, core, lax.rem(chip + d, CHIPS)], orv.at[k, d - 1], k, DIR_O, peer(d)).start()
        sent.append(remote(orv.at[k], orv.at[k], k, DIR_O, sib))

    def b2(k):
        remote(orv.at[k], orv.at[k], k, DIR_O, sib).wait_recv()
        total = ob[k, core, chip]
        for d in range(CHIPS - 1):
            total = total + orv[k, d]
        out_ref[k] = total

    stages = {
        "A0": a0, "A1": a1, "A2": a2, "A3": a3, "A4": a4, "A4b": a4b, "Z2": z2, "Z3": z3, "Z4": z4, "Z6": z6,
        "Z7": z7, "P1": p1, "Z8": z8, "P2": lambda k: product_two(k, 1),
        "Z9": z9, "P3": lambda k: product_two(k, 2), "Z11": z11, "B1": b1, "B2": b2,
        "x_load": lambda k: x_load(), "h_prep": lambda k: h_prep(), "x_prep": lambda k: x_prep(),
    }
    for name, k in ORDER:
        stages[name](k)
    for copy in sent:
        copy.wait_send()


def on_device(x_matrix, h_matrix, x_mask, h_mask, panel):
    n, slab = x_matrix.shape[0], 32 // CHUNKS
    part = (ROWS // 2, EDGE)
    f32, bf16 = jnp.float32, jnp.bfloat16
    vmem, hbm = pl.BlockSpec(memory_space=pltpu.VMEM), pl.BlockSpec(memory_space=pl.ANY)
    out = pl.pallas_call(
        kernel,
        out_shape=pltpu.VMEM((CHUNKS, slab, n), f32),
        in_specs=[hbm, hbm, hbm, hbm, pl.BlockSpec(memory_space=pltpu.SMEM)],
        out_specs=vmem,
        scratch_shapes=[
            pltpu.VMEM((8, 8), jnp.int32), pltpu.VMEM((8, 8), jnp.int32),
            pltpu.VMEM((2, CHIPS, 2, CHUNKS, slab, n), f32),
            pltpu.VMEM((n, n), f32),
            pltpu.VMEM((n, n), bf16), pltpu.VMEM((n, n), bf16),
            pltpu.VMEM((n, n), bf16), pltpu.VMEM((n, n), bf16),
            pltpu.VMEM((2, 4, n), f32), pltpu.VMEM((8, n), f32), pltpu.VMEM((8, n), f32),
            pltpu.VMEM((CHUNKS, 2, CHIPS, slab, n), f32),
            pltpu.VMEM((CHUNKS, CHIPS, slab, n), f32),
            pltpu.VMEM((CHUNKS, CHIPS - 1, slab, n), f32),
            pltpu.VMEM((CHUNKS, 2, CHIPS, slab, n), f32),
            pltpu.VMEM((CHUNKS, 2 * ROWS, n), bf16), pltpu.VMEM((2 * ROWS, 2 * EDGE), bf16),
            pltpu.VMEM((CHUNKS, RING, 2, *part), f32),
            pltpu.VMEM((CHUNKS, *part), f32), pltpu.VMEM((CHUNKS, *part), f32),
            pltpu.VMEM((CHUNKS, 2, *part), f32), pltpu.VMEM((CHUNKS, 2, *part), f32),
            pltpu.VMEM((CHUNKS, 2, *part), f32), pltpu.VMEM((CHUNKS, 2, *part), f32),
            pltpu.VMEM((CHUNKS, 2, *part), f32), pltpu.VMEM((CHUNKS, 3, *part), f32),
            pltpu.VMEM((CHUNKS, RING, 2, *part), f32),
            pltpu.VMEM((CHUNKS, 2, CHIPS, slab, n), f32),
            pltpu.VMEM((CHUNKS, CHIPS, slab, n), f32),
            pltpu.VMEM((CHUNKS, CHIPS - 1, slab, n), f32),
            pltpu.SemaphoreType.DMA((4,)),
            pltpu.SemaphoreType.DMA((CHUNKS, N_SEMS)),
            pltpu.SemaphoreType.DMA((CHUNKS, N_SEMS)),
        ],
        compiler_params=pltpu.CompilerParams(
            collective_id=0, has_side_effects=True, vmem_limit_bytes=56 * 1024 * 1024),
    )(x_matrix.reshape(2, CHIPS, 2, CHUNKS, slab, n), h_matrix, x_mask, h_mask, panel)
    return out.reshape(32, n)


def solution(mesh):
    return jax.shard_map(
        on_device,
        mesh=mesh,
        in_specs=(P("row", "col"), P("row", "col"), P("row", "col"), P("row", "col"), P()),
        out_specs=P("row", "col"),
        check_vma=False,
    )
```

```python
import functools

import jax
import jax.numpy as jnp
from jax import lax
from jax.experimental import pallas as pl
from jax.experimental.pallas import tpu as pltpu
from jax.sharding import PartitionSpec as P

MESH = pl.DeviceIdType.MESH
CHUNKS = 4
PANEL = 512
ROWS = PANEL // CHUNKS
CHIPS = 8
RING = 8
EDGE = 128
FAR_FIRST = (5, 3, 4, 7, 1, 2, 6)

SHORT_SUM = (0, 1, 2, 3)
SHORT_GATHER = (0, 1, 2, 3)

ORDER = (
    ("x_load", 0), ("A0", 0), ("A1", 0), ("A0", 2), ("A1", 2), ("A0", 1), ("A0", 3), ("A1", 1), ("A2", 0),
    ("h_prep", 0), ("A2", 2), ("A1", 3), ("A3", 0), ("A2", 1), ("A4", 0), ("A4b", 0), ("A3", 2), ("A4", 2),
    ("A2", 3), ("A3", 1), ("Z3", 0), ("A4", 1), ("A4b", 2), ("Z3", 2), ("A4b", 1), ("A3", 3), ("Z4", 0),
    ("A4", 3), ("A4b", 3), ("Z3", 1), ("Z4", 2), ("Z6", 0), ("x_prep", 0), ("Z3", 3), ("Z4", 1), ("Z6", 2),
    ("Z7", 0), ("Z4", 3), ("Z6", 1), ("Z7", 2), ("Z8", 0), ("Z6", 3), ("Z7", 1), ("Z8", 2), ("P1", 0), ("Z7", 3),
    ("P1", 2), ("P2", 0), ("Z11", 0), ("Z8", 1), ("P1", 1), ("P2", 2), ("B1", 0), ("Z11", 2), ("Z8", 3),
    ("P1", 3), ("P2", 3), ("B1", 2), ("P2", 1), ("Z11", 1), ("B1", 1), ("B2", 0), ("Z11", 3), ("B1", 3),
    ("B2", 1), ("B2", 2), ("B2", 3),
)

CORE_P, DIR_P, AG_P, CORE_R, CORE_O, DIR_O, OWN, HALF_U, HALF_D, LAST, FIRST, NEAR, PASS_U, PASS_D = range(14)
RU, RD, GU, GD = 14, 16, 18, 20
N_SEMS = 22


def kernel(x_hbm, h_hbm, xm_hbm, hm_hbm, panel_ref, out_ref,
           xm_ref, hm_ref, xv, hv, xh, xl, hh, hl, wx, mx, mh, piece, pc, pr, rr, ab, tb, tp, zu1, zd1, zu, zd, zhu, zhd, zl, yo, tf,
           ob, oc, orv, load_sem, send, recv):
    row, col = lax.axis_index("row"), lax.axis_index("col")
    core, chip = lax.rem(row, 2), lax.div(row, 2)
    z, ylo = lax.rem(col, RING), lax.div(col, RING)
    sib = (row + 1 - 2 * core, col)
    def at_z(d):
        return lax.rem(z + (d + RING) % RING, RING)

    other = 1 - ylo
    ypart = (row, other * RING + z)
    z_up, z_down = lax.rem(z + 1, RING), lax.rem(z + RING - 1, RING)
    up, up_other = (row, ylo * RING + z_up), (row, other * RING + z_up)
    down, down_other = (row, ylo * RING + z_down), (row, other * RING + z_down)
    up_two, down_two = (row, ylo * RING + at_z(2)), (row, ylo * RING + at_z(-2))
    around = [up_two, down_two, up, down, up_other, down_other, ypart]

    def peer(d):
        return (lax.rem(chip + d, CHIPS) * 2 + core, col)

    load_x = pltpu.make_async_copy(x_hbm, xv, load_sem.at[0])
    load_h = pltpu.make_async_copy(h_hbm, hv, load_sem.at[1])
    load_xm = pltpu.make_async_copy(xm_hbm, xm_ref, load_sem.at[2])
    load_hm = pltpu.make_async_copy(hm_hbm, hm_ref, load_sem.at[3])
    load_xm.start()
    load_x.start()
    load_hm.start()

    barrier = pltpu.get_barrier_semaphore()
    friends = [sib] + around + [peer(d) for d in range(1, CHIPS)]
    for friend in friends:
        pl.semaphore_signal(barrier, inc=1, device_id=friend, device_id_type=MESH)

    def remote(src, dst, k, sem, device):
        return pltpu.make_async_remote_copy(
            src_ref=src, dst_ref=dst, send_sem=send.at[k, sem], recv_sem=recv.at[k, sem],
            device_id=device, device_id_type=MESH)

    sent = []

    def push(src, dst, k, sem, device):
        copy = remote(src, dst, k, sem, device)
        copy.start()
        sent.append(copy)

    def spread(mask):
        m = mask.astype(jnp.float32)
        return jnp.concatenate(
            [jnp.broadcast_to(m[:, j:j + 1], (m.shape[0], EDGE)) for j in range(m.shape[1])], axis=1)

    def split(value):
        high = value.astype(jnp.bfloat16)
        return high, (value - high.astype(jnp.float32)).astype(jnp.bfloat16)

    def product_one(k, step):
        far = lax.div(at_z(4), 2)
        turn = 1 - 2 * lax.rem(z + 1, 2)
        pair = lax.rem(far + (0, 4 + turn, 4 - turn, 2)[step], 4)
        rows = pl.ds(pl.multiple_of(pair * 256, 256), 256)
        first = jnp.dot(ab[k], hh[:, rows], preferred_element_type=jnp.float32)
        second = jnp.dot(ab[k, 0:ROWS, :], hl[:, rows], preferred_element_type=jnp.float32)
        value = first[:ROWS] + (first[ROWS:] + second)
        tp[k, 2 * pair] = value[:, :EDGE].reshape(2, ROWS // 2, EDGE)
        tp[k, 2 * pair + 1] = value[:, EDGE:].reshape(2, ROWS // 2, EDGE)

    def product_two(k, step):
        turn = 1 - 2 * lax.rem(z + 1, 2)
        pair = lax.rem(lax.div(z, 2) + (0, 4 + turn, 4 - turn, 2)[step], 4)
        for half in range(2):
            a, b = split(tf[k, 2 * pair + half].reshape(ROWS, EDGE))
            tb[0:ROWS, half * EDGE:(half + 1) * EDGE] = a
            tb[ROWS:, half * EDGE:(half + 1) * EDGE] = b
        rows = pl.ds(pl.multiple_of(pair * 256, 256), 256)
        for n in range(0, 1024, 256):
            first = jnp.dot(tb[...], xh[rows, n:n + 256], preferred_element_type=jnp.float32)
            second = jnp.dot(tb[0:ROWS, :], xl[rows, n:n + 256], preferred_element_type=jnp.float32)
            value = (first[:ROWS] + (first[ROWS:] + second)).reshape(2, CHIPS, ROWS // 16, 256)
            ob[k, :, :, :, n:n + 256] = value if step == 0 else ob[k, :, :, :, n:n + 256] + value

    def x_load():
        load_xm.wait()
        mx[...] = spread(xm_ref[...])
        s0 = jnp.where(panel_ref[0] == 2 * row, 1.0, 0.0)
        s1 = jnp.where(panel_ref[0] == 2 * row + 1, 1.0, 0.0)
        wx[0] = mx[0:4, :] * s0
        wx[1] = mx[4:8, :] * s1
        load_x.wait()
        load_h.start()

    def h_prep():
        load_hm.wait()
        mh[...] = spread(hm_ref[...])
        load_h.wait()

        def body(b, carry):
            rows = pl.ds(pl.multiple_of(b * EDGE, EDGE), EDGE)
            high, low = split((hv[rows, :] * mh[pl.ds(b, 1), :]).T)
            hh[:, rows] = high
            hl[:, rows] = low
            return carry

        lax.fori_loop(0, 8, body, 0)

    def x_prep():
        def body(b, carry):
            rows = pl.ds(pl.multiple_of(b * EDGE, EDGE), EDGE)
            block = xv[lax.div(b, 4), pl.ds(lax.rem(b, 4) * 2, 2)].reshape(EDGE, 1024)
            high, low = split(block * mx[pl.ds(b, 1), :])
            xh[rows, :] = high
            xl[rows, :] = low
            return carry

        lax.fori_loop(0, 8, body, 0)

    def a0(k):
        for q in range(2):
            for g in range(CHIPS):
                w0, w1 = wx[0, g // 2:g // 2 + 1, :], wx[1, g // 2:g // 2 + 1, :]
                piece[k, q, g] = xv[0, g, q, k] * w0 + xv[1, g, q, k] * w1
        if not sent:
            pl.semaphore_wait(barrier, len(friends))
        push(piece.at[k, 1 - core], pc.at[k], k, CORE_P, sib)

    def a1(k):
        remote(pc.at[k], pc.at[k], k, CORE_P, sib).wait_recv()
        piece[k, core] = piece[k, core] + pc[k]
        for d in FAR_FIRST:
            remote(piece.at[k, core, lax.rem(chip + d, CHIPS)], pr.at[k, d - 1], k, DIR_P, peer(d)).start()
        sent.append(remote(pr.at[k], pr.at[k], k, DIR_P, sib))

    def a2(k):
        remote(pr.at[k], pr.at[k], k, DIR_P, sib).wait_recv()
        total = piece[k, core, chip]
        for d in range(CHIPS - 1):
            total = total + pr[k, d]
        rr[k, core, chip] = total
        for d in FAR_FIRST:
            remote(rr.at[k, core, chip], rr.at[k, core, chip], k, AG_P, peer(d)).start()
        sent.append(remote(pr.at[k], pr.at[k], k, AG_P, sib))

    def a3(k):
        remote(pr.at[k], pr.at[k], k, AG_P, sib).wait_recv()
        push(rr.at[k, core], rr.at[k, core], k, CORE_R, sib)

    def a4(k):
        remote(rr.at[k, core], rr.at[k, 1 - core], k, CORE_R, sib).wait_recv()
        high, low = split(rr[k].reshape(ROWS, 1024))
        ab[k, 0:ROWS, :] = high
        ab[k, ROWS:, :] = low
        product_one(k, 0)
        if k in SHORT_SUM:
            product_one(k, 1)
            push(tp.at[k, at_z(4), 0], zu1.at[k], k, RU, up_two)
            push(tp.at[k, at_z(4), 1], zd1.at[k], k, RD, down_two)
            push(tp.at[k, at_z(3)], zu.at[k], k, RU + 1, up)
            push(tp.at[k, at_z(-3)], zd.at[k], k, RD + 1, down)
        else:
            push(tp.at[k, at_z(4), 0], zu1.at[k], k, RU, up)
            push(tp.at[k, at_z(4), 1], zd1.at[k], k, RD, down)

    def a4b(k):
        for step in (2, 3) if k in SHORT_SUM else (1, 2, 3):
            product_one(k, step)
        for slot, owner in enumerate((z_up, z_down, z)):
            remote(tp.at[k, owner, other], yo.at[k, slot], k, OWN, ypart).start()
        sent.append(remote(yo.at[k], yo.at[k], k, OWN, ypart))

    def z2(k):
        remote(zu1.at[k], zu1.at[k], k, RU, up).wait_recv()
        tp[k, at_z(3), 0] = tp[k, at_z(3), 0] + zu1[k]
        push(tp.at[k, at_z(3)], zu.at[k], k, RU + 1, up)
        remote(zd1.at[k], zd1.at[k], k, RD, down).wait_recv()
        tp[k, at_z(-3), 1] = tp[k, at_z(-3), 1] + zd1[k]
        push(tp.at[k, at_z(-3)], zd.at[k], k, RD + 1, down)

    def z3(k):
        if k in SHORT_SUM:
            remote(zu1.at[k], zu1.at[k], k, RU, up).wait_recv()
            tp[k, at_z(2), 0] = tp[k, at_z(2), 0] + zu1[k]
            remote(zd1.at[k], zd1.at[k], k, RD, down).wait_recv()
            tp[k, at_z(-2), 1] = tp[k, at_z(-2), 1] + zd1[k]
        remote(zu.at[k], zu.at[k], k, RU + 1, up).wait_recv()
        tp[k, at_z(2)] = tp[k, at_z(2)] + zu[k]
        remote(tp.at[k, at_z(2), other], zhu.at[k, 1], k, HALF_U, up_other).start()
        remote(tp.at[k, at_z(2), ylo], zhu.at[k, 0], k, HALF_U, up).start()
        sent.append(remote(zhu.at[k], zhu.at[k], k, HALF_U, up))
        remote(zd.at[k], zd.at[k], k, RD + 1, down).wait_recv()
        tp[k, at_z(-2)] = tp[k, at_z(-2)] + zd[k]
        remote(tp.at[k, at_z(-2), other], zhd.at[k, 1], k, HALF_D, down_other).start()
        remote(tp.at[k, at_z(-2), ylo], zhd.at[k, 0], k, HALF_D, down).start()
        sent.append(remote(zhd.at[k], zhd.at[k], k, HALF_D, down))

    def z4(k):
        remote(yo.at[k], yo.at[k], k, OWN, ypart).wait_recv()
        remote(zhu.at[k], zhu.at[k], k, HALF_U, up).wait_recv()
        tp[k, z_up, ylo] = tp[k, z_up, ylo] + (yo[k, 0] + (zhu[k, 0] + zhu[k, 1]))
        remote(tp.at[k, z_up, ylo], zl.at[k, 0], k, LAST, up).start()
        remote(zhd.at[k], zhd.at[k], k, HALF_D, down).wait_recv()
        tp[k, z_down, ylo] = tp[k, z_down, ylo] + (yo[k, 1] + (zhd[k, 0] + zhd[k, 1]))
        remote(tp.at[k, z_down, ylo], zl.at[k, 1], k, LAST, down).start()
        sent.append(remote(zl.at[k], zl.at[k], k, LAST, up))

    def z6(k):
        remote(zl.at[k], zl.at[k], k, LAST, up).wait_recv()
        tf[k, z, ylo] = tp[k, z, ylo] + (yo[k, 2] + (zl[k, 0] + zl[k, 1]))
        for device in (up, down, ypart):
            remote(tf.at[k, z, ylo], tf.at[k, z, ylo], k, FIRST, device).start()
        sent.append(remote(yo.at[k], yo.at[k], k, FIRST, up))

    def z7(k):
        remote(yo.at[k], yo.at[k], k, FIRST, up).wait_recv()
        below, above = tf.at[k, z_down, ylo], tf.at[k, z_up, ylo]
        remote(below, below, k, PASS_U, up_other).start()
        remote(below, below, k, PASS_U, up).start()
        remote(above, above, k, PASS_D, down_other).start()
        remote(above, above, k, PASS_D, down).start()
        remote(below, below, k, NEAR, ypart).start()
        remote(above, above, k, NEAR, ypart).start()
        for sem in (PASS_U, PASS_D, NEAR):
            sent.append(remote(zl.at[k], zl.at[k], k, sem, up))

    def z8(k):
        below, above = tf.at[k, at_z(-2)], tf.at[k, at_z(2)]
        remote(zl.at[k], zl.at[k], k, PASS_U, up).wait_recv()
        if k in SHORT_GATHER:
            push(below.at[0], below.at[0], k, GU + 1, up_two)
        push(below, below, k, GU, up)
        remote(zl.at[k], zl.at[k], k, PASS_D, down).wait_recv()
        if k in SHORT_GATHER:
            push(above.at[1], above.at[1], k, GD + 1, down_two)
        push(above, above, k, GD, down)

    def p1(k):
        remote(zl.at[k], zl.at[k], k, NEAR, ypart).wait_recv()
        product_two(k, 0)

    def z9(k):
        below, above = at_z(-3), at_z(3)
        remote(tf.at[k, below], tf.at[k, below], k, GU, up).wait_recv()
        push(tf.at[k, below, 0], tf.at[k, below, 0], k, GU + 1, up)
        remote(tf.at[k, above], tf.at[k, above], k, GD, down).wait_recv()
        push(tf.at[k, above, 1], tf.at[k, above, 1], k, GD + 1, down)

    def z11(k):
        far = at_z(4)
        remote(tf.at[k, far, 0], tf.at[k, far, 0], k, GU + 1, up).wait_recv()
        remote(tf.at[k, far, 1], tf.at[k, far, 1], k, GD + 1, down).wait_recv()
        if k in SHORT_GATHER:
            below, above = at_z(-3), at_z(3)
            remote(tf.at[k, below], tf.at[k, below], k, GU, up).wait_recv()
            remote(tf.at[k, above], tf.at[k, above], k, GD, down).wait_recv()
            product_two(k, 2)
        product_two(k, 3)
        push(ob.at[k, 1 - core], oc.at[k], k, CORE_O, sib)

    def b1(k):
        remote(oc.at[k], oc.at[k], k, CORE_O, sib).wait_recv()
        ob[k, core] = ob[k, core] + oc[k]
        for d in FAR_FIRST:
            remote(ob.at[k, core, lax.rem(chip + d, CHIPS)], orv.at[k, d - 1], k, DIR_O, peer(d)).start()
        sent.append(remote(orv.at[k], orv.at[k], k, DIR_O, sib))

    def b2(k):
        remote(orv.at[k], orv.at[k], k, DIR_O, sib).wait_recv()
        total = ob[k, core, chip]
        for d in range(CHIPS - 1):
            total = total + orv[k, d]
        out_ref[k] = total

    stages = {
        "A0": a0, "A1": a1, "A2": a2, "A3": a3, "A4": a4, "A4b": a4b, "Z2": z2, "Z3": z3, "Z4": z4, "Z6": z6,
        "Z7": z7, "P1": p1, "Z8": z8, "P2": lambda k: product_two(k, 1),
        "Z9": z9, "P3": lambda k: product_two(k, 2), "Z11": z11, "B1": b1, "B2": b2,
        "x_load": lambda k: x_load(), "h_prep": lambda k: h_prep(), "x_prep": lambda k: x_prep(),
    }
    last = max(i for i, (name, _) in enumerate(ORDER) if name == "B1")
    for i, (name, k) in enumerate(ORDER):
        stages[name](k)
        if i == last:
            for copy in sent[:-1]:
                copy.wait_send()
            del sent[:-1]
    for copy in sent:
        copy.wait_send()


def on_device(x_matrix, h_matrix, x_mask, h_mask, panel):
    n, slab = x_matrix.shape[0], 32 // CHUNKS
    part = (ROWS // 2, EDGE)
    f32, bf16 = jnp.float32, jnp.bfloat16
    vmem, hbm = pl.BlockSpec(memory_space=pltpu.VMEM), pl.BlockSpec(memory_space=pl.ANY)
    out = pl.pallas_call(
        kernel,
        out_shape=pltpu.VMEM((CHUNKS, slab, n), f32),
        in_specs=[hbm, hbm, hbm, hbm, pl.BlockSpec(memory_space=pltpu.SMEM)],
        out_specs=vmem,
        scratch_shapes=[
            pltpu.VMEM((8, 8), jnp.int32), pltpu.VMEM((8, 8), jnp.int32),
            pltpu.VMEM((2, CHIPS, 2, CHUNKS, slab, n), f32),
            pltpu.VMEM((n, n), f32),
            pltpu.VMEM((n, n), bf16), pltpu.VMEM((n, n), bf16),
            pltpu.VMEM((n, n), bf16), pltpu.VMEM((n, n), bf16),
            pltpu.VMEM((2, 4, n), f32), pltpu.VMEM((8, n), f32), pltpu.VMEM((8, n), f32),
            pltpu.VMEM((CHUNKS, 2, CHIPS, slab, n), f32),
            pltpu.VMEM((CHUNKS, CHIPS, slab, n), f32),
            pltpu.VMEM((CHUNKS, CHIPS - 1, slab, n), f32),
            pltpu.VMEM((CHUNKS, 2, CHIPS, slab, n), f32),
            pltpu.VMEM((CHUNKS, 2 * ROWS, n), bf16), pltpu.VMEM((2 * ROWS, 2 * EDGE), bf16),
            pltpu.VMEM((CHUNKS, RING, 2, *part), f32),
            pltpu.VMEM((CHUNKS, *part), f32), pltpu.VMEM((CHUNKS, *part), f32),
            pltpu.VMEM((CHUNKS, 2, *part), f32), pltpu.VMEM((CHUNKS, 2, *part), f32),
            pltpu.VMEM((CHUNKS, 2, *part), f32), pltpu.VMEM((CHUNKS, 2, *part), f32),
            pltpu.VMEM((CHUNKS, 2, *part), f32), pltpu.VMEM((CHUNKS, 3, *part), f32),
            pltpu.VMEM((CHUNKS, RING, 2, *part), f32),
            pltpu.VMEM((CHUNKS, 2, CHIPS, slab, n), f32),
            pltpu.VMEM((CHUNKS, CHIPS, slab, n), f32),
            pltpu.VMEM((CHUNKS, CHIPS - 1, slab, n), f32),
            pltpu.SemaphoreType.DMA((4,)),
            pltpu.SemaphoreType.DMA((CHUNKS, N_SEMS)),
            pltpu.SemaphoreType.DMA((CHUNKS, N_SEMS)),
        ],
        compiler_params=pltpu.CompilerParams(
            collective_id=0, has_side_effects=True, vmem_limit_bytes=56 * 1024 * 1024),
    )(x_matrix.reshape(2, CHIPS, 2, CHUNKS, slab, n), h_matrix, x_mask, h_mask, panel)
    return out.reshape(32, n)


def solution(mesh):
    return jax.shard_map(
        on_device,
        mesh=mesh,
        in_specs=(P("row", "col"), P("row", "col"), P("row", "col"), P("row", "col"), P()),
        out_specs=P("row", "col"),
        check_vma=False,
    )
```

```python
import functools

import jax
import jax.numpy as jnp
from jax import lax
from jax.experimental import pallas as pl
from jax.experimental.pallas import tpu as pltpu
from jax.sharding import PartitionSpec as P

MESH = pl.DeviceIdType.MESH
CHUNKS = 4
PANEL = 512
ROWS = PANEL // CHUNKS
CHIPS = 8
RING = 8
EDGE = 128
FAR_FIRST = (5, 3, 4, 7, 1, 2, 6)

SHORT_SUM = (0, 1, 2, 3)
SHORT_GATHER = (0, 1, 2, 3)

ORDER = (
    ("x_load", 0), ("A0", 0), ("A1", 0), ("A0", 2), ("A1", 2), ("A0", 1), ("A0", 3), ("A1", 1), ("A2", 0),
    ("h_prep", 0), ("A2", 2), ("A1", 3), ("A3", 0), ("A2", 1), ("A4", 0), ("A4b", 0), ("A3", 2), ("A4", 2),
    ("A2", 3), ("A3", 1), ("Z3", 0), ("A4", 1), ("A4b", 2), ("Z3", 2), ("A4b", 1), ("A3", 3), ("Z4", 0),
    ("A4", 3), ("A4b", 3), ("Z3", 1), ("Z4", 2), ("Z6", 0), ("x_prep", 0), ("Z3", 3), ("Z4", 1), ("Z6", 2),
    ("Z7", 0), ("Z4", 3), ("Z6", 1), ("Z7", 2), ("Z8", 0), ("Z6", 3), ("Z7", 1), ("Z8", 2), ("P1", 0), ("Z7", 3),
    ("P1", 2), ("P2", 0), ("Z11", 0), ("Z8", 1), ("P1", 1), ("P2", 2), ("B1", 0), ("Z11", 2), ("Z8", 3),
    ("P1", 3), ("P2", 3), ("B1", 2), ("P2", 1), ("Z11", 1), ("B1", 1), ("B2", 0), ("Z11", 3), ("B1", 3),
    ("B2", 1), ("B2", 2), ("B2", 3),
)

CORE_P, DIR_P, AG_P, CORE_R, CORE_O, DIR_O, OWN, HALF_U, HALF_D, LAST, FIRST, NEAR, PASS_U, PASS_D = range(14)
RU, RD, GU, GD = 14, 16, 18, 20
N_SEMS = 22


def kernel(x_hbm, h_hbm, xm_hbm, hm_hbm, panel_ref, out_ref,
           xm_ref, hm_ref, xv, hv, xh, xl, hh, hl, wx, mx, mh, piece, pc, pr, rr, ab, tb, tp, zu1, zd1, zu, zd, zhu, zhd, zl, yo, tf,
           ob, oc, orv, load_sem, send, recv):
    row, col = lax.axis_index("row"), lax.axis_index("col")
    core, chip = lax.rem(row, 2), lax.div(row, 2)
    z, ylo = lax.rem(col, RING), lax.div(col, RING)
    sib = (row + 1 - 2 * core, col)
    def at_z(d):
        return lax.rem(z + (d + RING) % RING, RING)

    other = 1 - ylo
    ypart = (row, other * RING + z)
    z_up, z_down = lax.rem(z + 1, RING), lax.rem(z + RING - 1, RING)
    up, up_other = (row, ylo * RING + z_up), (row, other * RING + z_up)
    down, down_other = (row, ylo * RING + z_down), (row, other * RING + z_down)
    up_two, down_two = (row, ylo * RING + at_z(2)), (row, ylo * RING + at_z(-2))
    around = [up_two, down_two, up, down, up_other, down_other, ypart]

    def peer(d):
        return (lax.rem(chip + d, CHIPS) * 2 + core, col)

    load_x = pltpu.make_async_copy(x_hbm, xv, load_sem.at[0])
    load_h = pltpu.make_async_copy(h_hbm, hv, load_sem.at[1])
    load_xm = pltpu.make_async_copy(xm_hbm, xm_ref, load_sem.at[2])
    load_hm = pltpu.make_async_copy(hm_hbm, hm_ref, load_sem.at[3])
    load_xm.start()
    load_x.start()
    load_hm.start()

    barrier = pltpu.get_barrier_semaphore()
    friends = [sib] + around + [peer(d) for d in range(1, CHIPS)]
    for friend in friends:
        pl.semaphore_signal(barrier, inc=1, device_id=friend, device_id_type=MESH)

    def remote(src, dst, k, sem, device):
        return pltpu.make_async_remote_copy(
            src_ref=src, dst_ref=dst, send_sem=send.at[k, sem], recv_sem=recv.at[k, sem],
            device_id=device, device_id_type=MESH)

    sent = []

    def push(src, dst, k, sem, device):
        copy = remote(src, dst, k, sem, device)
        copy.start()
        sent.append(copy)

    def spread(mask):
        m = mask.astype(jnp.float32)
        return jnp.concatenate(
            [jnp.broadcast_to(m[:, j:j + 1], (m.shape[0], EDGE)) for j in range(m.shape[1])], axis=1)

    def split(value):
        high = value.astype(jnp.bfloat16)
        return high, (value - high.astype(jnp.float32)).astype(jnp.bfloat16)

    def product_one(k, step):
        far = lax.div(at_z(4), 2)
        turn = 1 - 2 * lax.rem(z + 1, 2)
        pair = lax.rem(far + (0, 4 + turn, 4 - turn, 2)[step], 4)
        rows = pl.ds(pl.multiple_of(pair * 256, 256), 256)
        first = jnp.dot(ab[k], hh[:, rows], preferred_element_type=jnp.float32)
        second = jnp.dot(ab[k, 0:ROWS, :], hl[:, rows], preferred_element_type=jnp.float32)
        value = first[:ROWS] + (first[ROWS:] + second)
        tp[k, 2 * pair] = value[:, :EDGE].reshape(2, ROWS // 2, EDGE)
        tp[k, 2 * pair + 1] = value[:, EDGE:].reshape(2, ROWS // 2, EDGE)

    def product_two(k, step, ready=None):
        turn = 1 - 2 * lax.rem(z + 1, 2)
        pair = lax.rem(lax.div(z, 2) + (0, 4 + turn, 4 - turn, 2)[step], 4)
        for half in range(2):
            a, b = split(tf[k, 2 * pair + half].reshape(ROWS, EDGE))
            tb[0:ROWS, half * EDGE:(half + 1) * EDGE] = a
            tb[ROWS:, half * EDGE:(half + 1) * EDGE] = b
        rows = pl.ds(pl.multiple_of(pair * 256, 256), 256)
        for n in range(0, 1024, 256):
            first = jnp.dot(tb[...], xh[rows, n:n + 256], preferred_element_type=jnp.float32)
            second = jnp.dot(tb[0:ROWS, :], xl[rows, n:n + 256], preferred_element_type=jnp.float32)
            value = (first[:ROWS] + (first[ROWS:] + second)).reshape(2, CHIPS, ROWS // 16, 256)
            ob[k, :, :, :, n:n + 256] = value if step == 0 else ob[k, :, :, :, n:n + 256] + value
            if ready is not None and n % 512 == 256:
                ready(n - 256)

    def x_load():
        load_xm.wait()
        mx[...] = spread(xm_ref[...])
        s0 = jnp.where(panel_ref[0] == 2 * row, 1.0, 0.0)
        s1 = jnp.where(panel_ref[0] == 2 * row + 1, 1.0, 0.0)
        wx[0] = mx[0:4, :] * s0
        wx[1] = mx[4:8, :] * s1
        load_x.wait()
        load_h.start()

    def h_prep():
        load_hm.wait()
        mh[...] = spread(hm_ref[...])
        load_h.wait()

        def body(b, carry):
            rows = pl.ds(pl.multiple_of(b * EDGE, EDGE), EDGE)
            high, low = split((hv[rows, :] * mh[pl.ds(b, 1), :]).T)
            hh[:, rows] = high
            hl[:, rows] = low
            return carry

        lax.fori_loop(0, 8, body, 0)

    def x_prep():
        def body(b, carry):
            rows = pl.ds(pl.multiple_of(b * EDGE, EDGE), EDGE)
            block = xv[lax.div(b, 4), pl.ds(lax.rem(b, 4) * 2, 2)].reshape(EDGE, 1024)
            high, low = split(block * mx[pl.ds(b, 1), :])
            xh[rows, :] = high
            xl[rows, :] = low
            return carry

        lax.fori_loop(0, 8, body, 0)

    def a0(k):
        for q in range(2):
            for g in range(CHIPS):
                w0, w1 = wx[0, g // 2:g // 2 + 1, :], wx[1, g // 2:g // 2 + 1, :]
                piece[k, q, g] = xv[0, g, q, k] * w0 + xv[1, g, q, k] * w1
        if not sent:
            pl.semaphore_wait(barrier, len(friends))
        push(piece.at[k, 1 - core], pc.at[k], k, CORE_P, sib)

    def a1(k):
        remote(pc.at[k], pc.at[k], k, CORE_P, sib).wait_recv()
        piece[k, core] = piece[k, core] + pc[k]
        for d in FAR_FIRST:
            remote(piece.at[k, core, lax.rem(chip + d, CHIPS)], pr.at[k, d - 1], k, DIR_P, peer(d)).start()
        sent.append(remote(pr.at[k], pr.at[k], k, DIR_P, sib))

    def a2(k):
        remote(pr.at[k], pr.at[k], k, DIR_P, sib).wait_recv()
        total = piece[k, core, chip]
        for d in range(CHIPS - 1):
            total = total + pr[k, d]
        rr[k, core, chip] = total
        for d in FAR_FIRST:
            remote(rr.at[k, core, chip], rr.at[k, core, chip], k, AG_P, peer(d)).start()
        sent.append(remote(pr.at[k], pr.at[k], k, AG_P, sib))

    def a3(k):
        remote(pr.at[k], pr.at[k], k, AG_P, sib).wait_recv()
        push(rr.at[k, core], rr.at[k, core], k, CORE_R, sib)

    def a4(k):
        remote(rr.at[k, core], rr.at[k, 1 - core], k, CORE_R, sib).wait_recv()
        high, low = split(rr[k].reshape(ROWS, 1024))
        ab[k, 0:ROWS, :] = high
        ab[k, ROWS:, :] = low
        product_one(k, 0)
        if k in SHORT_SUM:
            product_one(k, 1)
            push(tp.at[k, at_z(4), 0], zu1.at[k], k, RU, up_two)
            push(tp.at[k, at_z(4), 1], zd1.at[k], k, RD, down_two)
            push(tp.at[k, at_z(3)], zu.at[k], k, RU + 1, up)
            push(tp.at[k, at_z(-3)], zd.at[k], k, RD + 1, down)
        else:
            push(tp.at[k, at_z(4), 0], zu1.at[k], k, RU, up)
            push(tp.at[k, at_z(4), 1], zd1.at[k], k, RD, down)

    def a4b(k):
        for step in (2, 3) if k in SHORT_SUM else (1, 2, 3):
            product_one(k, step)
        for slot, owner in enumerate((z_up, z_down, z)):
            remote(tp.at[k, owner, other], yo.at[k, slot], k, OWN, ypart).start()
        sent.append(remote(yo.at[k], yo.at[k], k, OWN, ypart))

    def z2(k):
        remote(zu1.at[k], zu1.at[k], k, RU, up).wait_recv()
        tp[k, at_z(3), 0] = tp[k, at_z(3), 0] + zu1[k]
        push(tp.at[k, at_z(3)], zu.at[k], k, RU + 1, up)
        remote(zd1.at[k], zd1.at[k], k, RD, down).wait_recv()
        tp[k, at_z(-3), 1] = tp[k, at_z(-3), 1] + zd1[k]
        push(tp.at[k, at_z(-3)], zd.at[k], k, RD + 1, down)

    def z3(k):
        if k in SHORT_SUM:
            remote(zu1.at[k], zu1.at[k], k, RU, up).wait_recv()
            tp[k, at_z(2), 0] = tp[k, at_z(2), 0] + zu1[k]
            remote(zd1.at[k], zd1.at[k], k, RD, down).wait_recv()
            tp[k, at_z(-2), 1] = tp[k, at_z(-2), 1] + zd1[k]
        remote(zu.at[k], zu.at[k], k, RU + 1, up).wait_recv()
        tp[k, at_z(2)] = tp[k, at_z(2)] + zu[k]
        remote(tp.at[k, at_z(2), other], zhu.at[k, 1], k, HALF_U, up_other).start()
        remote(tp.at[k, at_z(2), ylo], zhu.at[k, 0], k, HALF_U, up).start()
        sent.append(remote(zhu.at[k], zhu.at[k], k, HALF_U, up))
        remote(zd.at[k], zd.at[k], k, RD + 1, down).wait_recv()
        tp[k, at_z(-2)] = tp[k, at_z(-2)] + zd[k]
        remote(tp.at[k, at_z(-2), other], zhd.at[k, 1], k, HALF_D, down_other).start()
        remote(tp.at[k, at_z(-2), ylo], zhd.at[k, 0], k, HALF_D, down).start()
        sent.append(remote(zhd.at[k], zhd.at[k], k, HALF_D, down))

    def z4(k):
        remote(yo.at[k], yo.at[k], k, OWN, ypart).wait_recv()
        remote(zhu.at[k], zhu.at[k], k, HALF_U, up).wait_recv()
        tp[k, z_up, ylo] = tp[k, z_up, ylo] + (yo[k, 0] + (zhu[k, 0] + zhu[k, 1]))
        remote(tp.at[k, z_up, ylo], zl.at[k, 0], k, LAST, up).start()
        remote(zhd.at[k], zhd.at[k], k, HALF_D, down).wait_recv()
        tp[k, z_down, ylo] = tp[k, z_down, ylo] + (yo[k, 1] + (zhd[k, 0] + zhd[k, 1]))
        remote(tp.at[k, z_down, ylo], zl.at[k, 1], k, LAST, down).start()
        sent.append(remote(zl.at[k], zl.at[k], k, LAST, up))

    def z6(k):
        remote(zl.at[k], zl.at[k], k, LAST, up).wait_recv()
        tf[k, z, ylo] = tp[k, z, ylo] + (yo[k, 2] + (zl[k, 0] + zl[k, 1]))
        for device in (up, down, ypart):
            remote(tf.at[k, z, ylo], tf.at[k, z, ylo], k, FIRST, device).start()
        sent.append(remote(yo.at[k], yo.at[k], k, FIRST, up))

    def z7(k):
        remote(yo.at[k], yo.at[k], k, FIRST, up).wait_recv()
        below, above = tf.at[k, z_down, ylo], tf.at[k, z_up, ylo]
        remote(below, below, k, PASS_U, up_other).start()
        remote(below, below, k, PASS_U, up).start()
        remote(above, above, k, PASS_D, down_other).start()
        remote(above, above, k, PASS_D, down).start()
        remote(below, below, k, NEAR, ypart).start()
        remote(above, above, k, NEAR, ypart).start()
        for sem in (PASS_U, PASS_D, NEAR):
            sent.append(remote(zl.at[k], zl.at[k], k, sem, up))

    def z8(k):
        below, above = tf.at[k, at_z(-2)], tf.at[k, at_z(2)]
        remote(zl.at[k], zl.at[k], k, PASS_U, up).wait_recv()
        if k in SHORT_GATHER:
            push(below.at[0], below.at[0], k, GU + 1, up_two)
        push(below, below, k, GU, up)
        remote(zl.at[k], zl.at[k], k, PASS_D, down).wait_recv()
        if k in SHORT_GATHER:
            push(above.at[1], above.at[1], k, GD + 1, down_two)
        push(above, above, k, GD, down)

    def p1(k):
        remote(zl.at[k], zl.at[k], k, NEAR, ypart).wait_recv()
        product_two(k, 0)

    def z9(k):
        below, above = at_z(-3), at_z(3)
        remote(tf.at[k, below], tf.at[k, below], k, GU, up).wait_recv()
        push(tf.at[k, below, 0], tf.at[k, below, 0], k, GU + 1, up)
        remote(tf.at[k, above], tf.at[k, above], k, GD, down).wait_recv()
        push(tf.at[k, above, 1], tf.at[k, above, 1], k, GD + 1, down)

    def z11(k):
        far = at_z(4)
        remote(tf.at[k, far, 0], tf.at[k, far, 0], k, GU + 1, up).wait_recv()
        remote(tf.at[k, far, 1], tf.at[k, far, 1], k, GD + 1, down).wait_recv()
        if k in SHORT_GATHER:
            below, above = at_z(-3), at_z(3)
            remote(tf.at[k, below], tf.at[k, below], k, GU, up).wait_recv()
            remote(tf.at[k, above], tf.at[k, above], k, GD, down).wait_recv()
            product_two(k, 2)

        def half(n):
            remote(ob.at[k, 1 - core, :, :, n:n + 512], oc.at[k, :, :, n:n + 512], k, CORE_O, sib).start()

        product_two(k, 3, half)
        sent.append(remote(oc.at[k], oc.at[k], k, CORE_O, sib))

    def b1(k):
        remote(oc.at[k], oc.at[k], k, CORE_O, sib).wait_recv()
        ob[k, core] = ob[k, core] + oc[k]
        for d in FAR_FIRST:
            remote(ob.at[k, core, lax.rem(chip + d, CHIPS)], orv.at[k, d - 1], k, DIR_O, peer(d)).start()
        sent.append(remote(orv.at[k], orv.at[k], k, DIR_O, sib))

    def b2(k):
        remote(orv.at[k], orv.at[k], k, DIR_O, sib).wait_recv()
        total = ob[k, core, chip]
        for d in range(CHIPS - 1):
            total = total + orv[k, d]
        out_ref[k] = total

    stages = {
        "A0": a0, "A1": a1, "A2": a2, "A3": a3, "A4": a4, "A4b": a4b, "Z2": z2, "Z3": z3, "Z4": z4, "Z6": z6,
        "Z7": z7, "P1": p1, "Z8": z8, "P2": lambda k: product_two(k, 1),
        "Z9": z9, "P3": lambda k: product_two(k, 2), "Z11": z11, "B1": b1, "B2": b2,
        "x_load": lambda k: x_load(), "h_prep": lambda k: h_prep(), "x_prep": lambda k: x_prep(),
    }
    last = max(i for i, (name, _) in enumerate(ORDER) if name == "B1")
    for i, (name, k) in enumerate(ORDER):
        stages[name](k)
        if i == last:
            for copy in sent[:-1]:
                copy.wait_send()
            del sent[:-1]
    for copy in sent:
        copy.wait_send()


def on_device(x_matrix, h_matrix, x_mask, h_mask, panel):
    n, slab = x_matrix.shape[0], 32 // CHUNKS
    part = (ROWS // 2, EDGE)
    f32, bf16 = jnp.float32, jnp.bfloat16
    vmem, hbm = pl.BlockSpec(memory_space=pltpu.VMEM), pl.BlockSpec(memory_space=pl.ANY)
    out = pl.pallas_call(
        kernel,
        out_shape=pltpu.VMEM((CHUNKS, slab, n), f32),
        in_specs=[hbm, hbm, hbm, hbm, pl.BlockSpec(memory_space=pltpu.SMEM)],
        out_specs=vmem,
        scratch_shapes=[
            pltpu.VMEM((8, 8), jnp.int32), pltpu.VMEM((8, 8), jnp.int32),
            pltpu.VMEM((2, CHIPS, 2, CHUNKS, slab, n), f32),
            pltpu.VMEM((n, n), f32),
            pltpu.VMEM((n, n), bf16), pltpu.VMEM((n, n), bf16),
            pltpu.VMEM((n, n), bf16), pltpu.VMEM((n, n), bf16),
            pltpu.VMEM((2, 4, n), f32), pltpu.VMEM((8, n), f32), pltpu.VMEM((8, n), f32),
            pltpu.VMEM((CHUNKS, 2, CHIPS, slab, n), f32),
            pltpu.VMEM((CHUNKS, CHIPS, slab, n), f32),
            pltpu.VMEM((CHUNKS, CHIPS - 1, slab, n), f32),
            pltpu.VMEM((CHUNKS, 2, CHIPS, slab, n), f32),
            pltpu.VMEM((CHUNKS, 2 * ROWS, n), bf16), pltpu.VMEM((2 * ROWS, 2 * EDGE), bf16),
            pltpu.VMEM((CHUNKS, RING, 2, *part), f32),
            pltpu.VMEM((CHUNKS, *part), f32), pltpu.VMEM((CHUNKS, *part), f32),
            pltpu.VMEM((CHUNKS, 2, *part), f32), pltpu.VMEM((CHUNKS, 2, *part), f32),
            pltpu.VMEM((CHUNKS, 2, *part), f32), pltpu.VMEM((CHUNKS, 2, *part), f32),
            pltpu.VMEM((CHUNKS, 2, *part), f32), pltpu.VMEM((CHUNKS, 3, *part), f32),
            pltpu.VMEM((CHUNKS, RING, 2, *part), f32),
            pltpu.VMEM((CHUNKS, 2, CHIPS, slab, n), f32),
            pltpu.VMEM((CHUNKS, CHIPS, slab, n), f32),
            pltpu.VMEM((CHUNKS, CHIPS - 1, slab, n), f32),
            pltpu.SemaphoreType.DMA((4,)),
            pltpu.SemaphoreType.DMA((CHUNKS, N_SEMS)),
            pltpu.SemaphoreType.DMA((CHUNKS, N_SEMS)),
        ],
        compiler_params=pltpu.CompilerParams(
            collective_id=0, has_side_effects=True, vmem_limit_bytes=56 * 1024 * 1024),
    )(x_matrix.reshape(2, CHIPS, 2, CHUNKS, slab, n), h_matrix, x_mask, h_mask, panel)
    return out.reshape(32, n)


def solution(mesh):
    return jax.shard_map(
        on_device,
        mesh=mesh,
        in_specs=(P("row", "col"), P("row", "col"), P("row", "col"), P("row", "col"), P()),
        out_specs=P("row", "col"),
        check_vma=False,
    )
```
